256 devices in a mesh: heads: 8 (over y, core), seq: 32 (over x, z).
Axes of the slice: x: 4, y: 4, z: 8, core: 2. Of those that a mesh axis runs over, the one named last changes fastest.
Arguments:
- queries: bfloat16 [8192, 1024], P(('seq', 'heads')), may hold values from -0.75 to 0.75
- keys: bfloat16 [8192, 1024], P(('seq', 'heads')), may hold values from -0.75 to 0.75
- values: bfloat16 [8192, 1024], P(('seq', 'heads')), may hold values from -6 to 6
- out_grad: bfloat16 [8192, 1024], P(('seq', 'heads')), may hold values from -0.0625 to 0.0625
- prefix_state: bfloat16 [32, 2080, 1024], P('seq', None, 'heads'), may hold values from -48 to 48
- variant_queries: bfloat16 [256, 1024], P('seq', 'heads'), may hold values from -0.75 to 0.75
- variant_grads: bfloat16 [256, 1024], P('seq', 'heads'), may hold values from -0.25 to 0.25
- variant_owner: int32 [256], replicated, may hold values from 0 to 31
- variant_position: int32 [256], replicated, may hold values from 0 to 255
- doc_start: int32 [32], P('seq'), may hold values from 1 to 256, as said below
Outputs:
- query_grad: float32 [8192, 1024], P(('seq', 'heads'))
- key_grad: float32 [8192, 1024], P(('seq', 'heads'))
- value_grad: float32 [8192, 1024], P(('seq', 'heads'))
The draws below stay inside these ranges and needn't reach their ends.
Inputs may be any that keep to these rules, and one draw needn't show every extreme that they name: `doc_start`: a document starts at this local position of the shard; 256 means that none starts inside it. `variant_position`: the local position in that shard at which the variant row stands.
All inputs are finite; a program needn't handle non-finite values.
Results may differ from the reference program's by a relative error of at most 0.004.
Values may be sent and summed in bfloat16 or wider, within the bound.
No kernel may reach another device: no remote copies, remote signals or barrier semaphores. Data moves between devices by JAX's collectives and lax.ppermute only.
A program may use at most 128 MiB of HBM per device.

```python
import math
import jax
import jax.numpy as jnp
from jax import lax

HEADS = 16
HEAD = 64
D = 1024
FEAT = 2080
TOK = 256
TOKENS = 8192
VARS = 256


def draw_doc_start(key, part):
    choose_key, spot_key, order_key = jax.random.split(jax.random.fold_in(key, 11), 3)
    count = TOKENS // TOK
    rolls = jax.random.randint(choose_key, (count,), 0, 4)
    spots = jax.random.randint(spot_key, (count,), 1, TOK)
    starts = jnp.where(rolls == 0, spots, TOK)
    order = jax.random.permutation(order_key, count)
    starts = starts.at[order[0]].set(1)
    starts = starts.at[order[1]].set(TOK)
    return starts.astype(jnp.int32)


def plant(values, stream_key, low, top_value):
    longest = values.shape.index(max(values.shape))
    spots = []
    for shift in (0, 1):
        where = [jax.random.randint(jax.random.fold_in(stream_key, axis), (), 0, length) for axis, length in enumerate(values.shape)]
        where[longest] = (where[longest] + shift) % values.shape[longest]
        spots.append(tuple(where))
    return values.at[spots[0]].set(low).at[spots[1]].set(top_value)


def block_scale(stream_key, extent, cuts, least, largest):
    gain, own = 1.0, jax.random.fold_in(stream_key, 6)
    for position, blocks in cuts:
        heights = jnp.exp(jax.random.uniform(jax.random.fold_in(own, position), (blocks,), jnp.float32, least / len(cuts), largest / len(cuts)))
        gain = gain * jnp.repeat(heights, extent[position] // blocks).reshape([-1 if axis == position else 1 for axis in range(len(extent))])
    return gain


def noise(rng, extent, spread, bound, cuts=(), kind=jnp.bfloat16):
    gain = block_scale(rng, extent, cuts, -0.22, 0.18) if cuts else 1.0
    values = jax.random.normal(rng, extent, jnp.float32) * spread * gain
    return jnp.minimum(jnp.maximum(values, -bound), bound).astype(kind)


def setup_inputs(seed: int = 0) -> dict:
    splits = jax.random.split(jax.random.key(seed), 11)
    queries = noise(splits[0], (TOKENS, D), (HEAD ** -0.5), 0.75, ((0, 256),))
    keys = noise(splits[1], (TOKENS, D), (HEAD ** -0.5), 0.75, ((0, 256),))
    values = noise(splits[2], (TOKENS, D), 1.0, 6.0, ((0, 256),))
    out_grad = noise(splits[3], (TOKENS, D), (TOKENS ** -0.5), 0.0625, ((0, 256),))
    prefix_state = noise(splits[4], (TOKENS // TOK, FEAT, D), 8.0, 48.0, ((0, 32), (2, 8)))
    variant_queries = noise(splits[5], (VARS, D), (HEAD ** -0.5), 0.75, ((0, 32), (1, 8)))
    variant_grads = noise(splits[6], (VARS, D), (4 * TOKENS ** -0.5), 0.25, ((0, 32), (1, 8)))
    variant_owner = plant(jax.random.randint(splits[7], (VARS,), 0, TOKENS // TOK), jax.random.fold_in(splits[7], 1), 0, (TOKENS // TOK) - 1).astype(jnp.int32)
    variant_position = plant(jax.random.randint(splits[8], (VARS,), 0, TOK), jax.random.fold_in(splits[8], 1), 0, TOK - 1).astype(jnp.int32)
    doc_start = draw_doc_start(jax.random.fold_in(splits[10], 71), 0)
    return {"queries": queries, "keys": keys, "values": values, "out_grad": out_grad, "prefix_state": prefix_state, "variant_queries": variant_queries, "variant_grads": variant_grads, "variant_owner": variant_owner, "variant_position": variant_position, "doc_start": doc_start}


def product(left, right):
    return jnp.dot(left.astype(jnp.float32), right.astype(jnp.float32), preferred_element_type=jnp.float32)

def expand(wide):
    width = wide.shape[1]
    pieces = []
    for first in range(width):
        count = width - first
        weights = jnp.where(jnp.arange(count) == 0, 1.0, math.sqrt(2.0)).astype(wide.dtype)
        pieces.append(wide[:, first:first + 1] * wide[:, first:] * weights)
    return jnp.concatenate(pieces, 1)

def features(rows):
    return expand(rows.astype(jnp.float32)).astype(jnp.bfloat16)

def state_grad(rows, grads, state):
    packed = product(grads, state.T)
    unused, pullback = jax.vjp(expand, rows.astype(packed.dtype))
    return pullback(packed)[0]

def attend(rows, grads, spots, live, keys, values, start):
    places = jnp.arange(keys.shape[0], dtype=jnp.int32)
    scores = product(rows, keys.T)
    inner = product(grads, values.T)
    seen = (places[None, :] <= spots[:, None]) & ((places[None, :] >= start) == (spots[:, None] >= start)) & live[:, None]
    slope = jnp.where(seen, 2.0 * scores * inner, 0.0).astype(jnp.bfloat16)
    square = jnp.where(seen, scores * scores, 0.0).astype(jnp.bfloat16)
    row_part = product(slope, keys)
    key_part = product(slope.T, rows)
    value_part = product(square.T, grads)
    return (row_part, key_part, value_part)

def reference(queries, keys, values, out_grad, prefix_state, variant_queries, variant_grads, variant_owner, variant_position, doc_start):
    shards = TOKENS // TOK

    def by_head(array):
        return jnp.transpose(array.reshape(shards, TOK, HEADS, HEAD), (2, 0, 1, 3))
    head_states = jnp.transpose(prefix_state.reshape(shards, FEAT, HEADS, HEAD), (2, 0, 1, 3))
    var_queries = jnp.transpose(variant_queries.reshape(VARS, HEADS, HEAD), (1, 0, 2))
    var_grads = jnp.transpose(variant_grads.reshape(VARS, HEADS, HEAD), (1, 0, 2))
    positions = jnp.arange(TOK, dtype=jnp.int32)
    shard_ids = jnp.arange(shards, dtype=jnp.int32)
    everyone = jnp.ones((TOK,), bool)

    def one_head(inputs):
        head_q, head_k, head_v, head_g, head_state, var_q, var_g = inputs

        def local_part(items):
            shard_q, shard_k, shard_v, shard_g, shard_state, start, shard = items
            before = positions < start
            intra_q, intra_k, intra_v = attend(shard_q, shard_g, positions, everyone, shard_k, shard_v, start)
            live = variant_owner == shard
            reads = live & (variant_position < start)
            unused, more_k, more_v = attend(var_q, var_g, variant_position, live, shard_k, shard_v, start)
            state_q = jnp.where(before[:, None], state_grad(shard_q, shard_g, shard_state), 0.0)
            own = product(features(shard_q).T, jnp.where(before[:, None], shard_g, 0))
            own = own + product(features(var_q).T, jnp.where(reads[:, None], var_g, 0))
            passes = jnp.where(start == TOK, 1.0, 0.0).astype(own.dtype)
            return (own, passes, intra_q + state_q, intra_k + more_k, intra_v + more_v)
        own, passes, grad_q, grad_k, grad_v = lax.map(local_part, (head_q, head_k, head_v, head_g, head_state, doc_start, shard_ids))

        def carry_back(later, items):
            step_own, step_pass = items
            return (step_own + step_pass * later, later)
        unused, later = lax.scan(carry_back, jnp.zeros((FEAT, HEAD), own.dtype), (own, passes), reverse=True)

        def state_part(items):
            shard_k, shard_v, shard_later, start = items
            carries = (positions >= start) | (start == TOK)
            later_bf = shard_later.astype(jnp.bfloat16)
            state_v = jnp.where(carries[:, None], product(features(shard_k), later_bf), 0.0)
            state_k = jnp.where(carries[:, None], state_grad(shard_k, shard_v, later_bf), 0.0)
            return (state_k, state_v)
        state_k, state_v = lax.map(state_part, (head_k, head_v, later, doc_start))
        return (grad_q, grad_k + state_k, grad_v + state_v)
    grad_q, grad_k, grad_v = lax.map(one_head, (by_head(queries), by_head(keys), by_head(values), by_head(out_grad), head_states, var_queries, var_grads))

    def back(array):
        return jnp.transpose(array, (1, 2, 0, 3)).reshape(TOKENS, D)
    return (back(grad_q), back(grad_k), back(grad_v))
```

```python
import functools
import math

import jax
import jax.numpy as jnp
from jax import lax
from jax.experimental import pallas as pl
from jax.experimental.pallas import tpu as pltpu
from jax.sharding import PartitionSpec as P

HEAD = 64
PAIR = 128
TOK = 256
FEAT = 2080
SHARDS = 32
ROW = 8
COLS = SHARDS // ROW
REACH = 8
F32 = jnp.float32
BF16 = jnp.bfloat16
I32 = jnp.int32

VMEM = pl.BlockSpec(memory_space=pltpu.VMEM)
SMEM = pl.BlockSpec(memory_space=pltpu.SMEM)


def call(body, out_shape, in_specs, out_specs, flops, scratch=(), aliases=None, name=None):
    return pl.pallas_call(
        body,
        out_shape=out_shape,
        in_specs=in_specs,
        out_specs=out_specs,
        scratch_shapes=list(scratch),
        input_output_aliases=aliases or {},
        compiler_params=pltpu.CompilerParams(vmem_limit_bytes=24 * 1024 * 1024),
        cost_estimate=pl.CostEstimate(flops=flops, bytes_accessed=1 << 20, transcendentals=0),
        name=name,
    )


def dot_nt(a, b):
    return lax.dot_general(a, b, (((1,), (1,)), ((), ())), preferred_element_type=F32)


def dot_tn(a, b):
    return lax.dot_general(a, b, (((0,), (0,)), ((), ())), preferred_element_type=F32)


def dot_nn(a, b):
    return lax.dot_general(a, b, (((1,), (0,)), ((), ())), preferred_element_type=F32)


def by_head(x):
    low = lax.broadcasted_iota(I32, x.shape, 1) < HEAD
    zero = jnp.zeros_like(x)
    return jnp.where(low, x, zero), jnp.where(low, zero, x)


def attend(q, g, keys, values, lo, hi):
    place = lax.broadcasted_iota(I32, (TOK, q.shape[0]), 0)
    seen = (place >= lo) & (place <= hi)
    slopes, squares = [], []
    for k, v in zip(by_head(keys), by_head(values)):
        score = jnp.where(seen, dot_nt(k, q), 0.0)
        inner = dot_nt(v, g)
        slopes.append((2.0 * score * inner).astype(BF16))
        squares.append((score * score).astype(BF16))
    slope = jnp.concatenate(slopes, 1)
    square = jnp.concatenate(squares, 1)
    k_part = dot_nn(slope, jnp.concatenate(by_head(q), 0))
    v_part = dot_nn(square, jnp.concatenate(by_head(g), 0))
    return slopes, k_part, v_part


def pack_body(q, g, k, v, vq, vg, scal, out, msg):
    for h in range(out.shape[0]):
        for n, ref in enumerate((q, g, k, v)):
            out[h, :, n * PAIR : (n + 1) * PAIR] = ref[:, h * PAIR : (h + 1) * PAIR]
    top = jnp.concatenate([vq[...], vg[...]], 1).astype(F32)
    start = jnp.full((8, 2 * PAIR), scal[1].astype(F32))
    msg[...] = jnp.concatenate([top, start], 0).astype(BF16)


def unpack_body(x, qo, ko, vo):
    for h in range(x.shape[0]):
        for n, ref in enumerate((qo, ko, vo)):
            ref[:, h * PAIR : (h + 1) * PAIR] = x[h, :, n * PAIR : (n + 1) * PAIR]


def own_body(scal, t, acc):
    start = scal[1]
    spot = lax.broadcasted_iota(I32, (1, TOK), 1)
    lo = jnp.where(spot >= start, start, 0)
    q, g, k, v = (t[:, n * PAIR : (n + 1) * PAIR] for n in range(4))
    slopes, k_part, v_part = attend(q, g, k, v, lo, spot)
    k0, k1 = by_head(k)
    acc[:, 0:PAIR] = dot_tn(slopes[0], k0) + dot_tn(slopes[1], k1)
    acc[:, PAIR : 2 * PAIR] = k_part
    acc[:, 2 * PAIR : 3 * PAIR] = v_part


def state_body(scal, m, t, acc_in, acc, pt, qt, rows, res):
    start = scal[1]
    chunk = 416
    for h, g in enumerate(by_head(t[:, PAIR : 2 * PAIR])):
        for c in range(0, FEAT, chunk):
            r = dot_nt(m[c : c + chunk, :], g)
            pt[2 * h, c : c + chunk, :] = r[:, 0:PAIR]
            pt[2 * h + 1, c : c + chunk, :] = r[:, PAIR : 2 * PAIR]
    q_t = t[:, 0:PAIR].astype(F32).T
    for h in range(2):
        for half in range(2):
            qt[2 * h + half] = q_t[h * HEAD : (h + 1) * HEAD, half * PAIR : (half + 1) * PAIR]
    sub = lax.broadcasted_iota(I32, (8, PAIR), 0)

    def part(i, carry):
        tiles = HEAD // 8
        sums = [jnp.zeros((8, PAIR), F32) for _ in range(tiles)]
        for a in range(HEAD):
            first = a // 8
            at = a * HEAD - a * (a - 1) // 2 - a % 8
            qa = qt[i, a : a + 1, :]
            row = None
            for b in range(first, tiles):
                tile = pt[i, at + 8 * (b - first) : at + 8 * (b - first) + 8, :]
                if b == first:
                    scale = jnp.where(sub > a % 8, 1.0, jnp.where(sub == a % 8, math.sqrt(0.5), 0.0))
                    tile = tile * scale
                sums[b] = sums[b] + tile * qa
                more = tile * qt[i, 8 * b : 8 * b + 8, :]
                row = more if row is None else row + more
            rows[i, a : a + 1, :] = jnp.sum(row, axis=0, keepdims=True)
        for b in range(tiles):
            res[i, 8 * b : 8 * b + 8, :] = math.sqrt(2.0) * (sums[b] + rows[i, 8 * b : 8 * b + 8, :])
        return carry

    lax.fori_loop(0, 4, part, 0)
    for half in range(2):
        both = jnp.concatenate([res[half], res[2 + half]], 0).T
        spot = half * PAIR + lax.broadcasted_iota(I32, (PAIR, PAIR), 0)
        at = slice(half * PAIR, (half + 1) * PAIR)
        acc[at, 0:PAIR] = acc_in[at, 0:PAIR] + jnp.where(spot < start, both, 0.0)
    acc[:, PAIR : 3 * PAIR] = acc_in[:, PAIR : 3 * PAIR]


def variant_body(scal, owner_ref, place_ref, t, acc_in, *rest):
    zrefs = rest[:ROW]
    acc, meta, rows, starts = rest[ROW:]
    shard = scal[0]
    start = scal[1]
    x, z = lax.div(shard, ROW), lax.rem(shard, ROW)
    for dz in range(ROW):
        block = zrefs[dz][...].astype(F32)
        for dx in range(COLS):
            at = lax.rem(x + dx, COLS) * ROW + lax.rem(z + dz, ROW)
            rows[pl.ds(pl.multiple_of(at * 8, 8), 8), :] = block[16 * dx : 16 * dx + 8, :]
            starts[pl.ds(at, 1), :] = block[16 * dx + 8 : 16 * dx + 9, :]
    begin = starts[...]
    sub = lax.broadcasted_iota(I32, (SHARDS, TOK), 0)
    lane = lax.broadcasted_iota(I32, (SHARDS, TOK), 1)
    along = jnp.sum(jnp.where(sub == lane, begin, 0.0), axis=0, keepdims=True)
    stops = (lane > sub) & (lane < SHARDS) & (along < TOK)
    last = jnp.min(jnp.where(stops, lane, SHARDS - 1).astype(F32), axis=1, keepdims=True)
    sub1 = lax.broadcasted_iota(I32, (SHARDS, 1), 0)
    longest = jnp.max(last - sub1.astype(F32)).astype(I32)
    mine = jnp.sum(jnp.where(sub1 == shard, last, 0.0)).astype(I32)
    final = jnp.sum(jnp.where(sub1 == mine, begin[:, 0:1], 0.0)).astype(I32)
    meta[0] = mine - shard
    meta[1] = final
    meta[2] = longest
    owner = owner_ref[...]
    place = place_ref[...]
    theirs = jnp.sum(jnp.where(sub == owner, begin, 0.0), axis=0, keepdims=True).astype(I32)
    here = owner == shard
    after = (owner > shard) & (owner <= mine) & (place < theirs)
    carry_lo = jnp.where(start == TOK, 0, start)
    lo = jnp.where(here, jnp.where(place >= start, start, 0), jnp.where(after, carry_lo, 1))
    hi = jnp.where(here, place, jnp.where(after, TOK - 1, 0))
    hi = jnp.where(here | after, hi, -1)
    both = rows[...].astype(BF16)
    k, v = t[:, 2 * PAIR : 3 * PAIR], t[:, 3 * PAIR : 4 * PAIR]
    _, k_part, v_part = attend(both[:, 0:PAIR], both[:, PAIR:], k, v, lo, hi)
    acc[:, 0:PAIR] = acc_in[:, 0:PAIR]
    acc[:, PAIR : 2 * PAIR] = acc_in[:, PAIR : 2 * PAIR] + k_part
    acc[:, 2 * PAIR : 3 * PAIR] = acc_in[:, 2 * PAIR : 3 * PAIR] + v_part


def later_block(far, scal, meta, t, block, acc):
    start = scal[1]

    @pl.when(far <= meta[0])
    def _():
        until = jnp.where(far == meta[0], meta[1], TOK)
        spot = lax.broadcasted_iota(I32, (1, TOK), 1)
        lo = jnp.where(start == TOK, 0, start)
        hi = jnp.where(spot < until, TOK - 1, -1)
        k, v = t[:, 2 * PAIR : 3 * PAIR], t[:, 3 * PAIR : 4 * PAIR]
        q, g = block[:, 0:PAIR], block[:, PAIR : 2 * PAIR]
        _, k_part, v_part = attend(q, g, k, v, lo, hi)
        acc[:, PAIR : 2 * PAIR] += k_part
        acc[:, 2 * PAIR : 3 * PAIR] += v_part


def later_body(fars, scal, meta, t, acc_in, *rest):
    blocks, acc = rest[:-1], rest[-1]
    acc[...] = acc_in[...]
    for far, block in zip(fars, blocks):
        later_block(far, scal, meta, t, block, acc)


def further_body(scal, meta, base, t, acc_in, blocks, acc):
    acc[...] = acc_in[...]
    for n in range(REACH // 2):
        later_block(base[0] + n + 1, scal, meta, t, blocks.at[n * TOK : (n + 1) * TOK, :], acc)


ACC = jax.ShapeDtypeStruct((TOK, 3 * PAIR), F32)
BLOCK_FLOPS = 8 * 2 * TOK * TOK * PAIR


def later_call(fars, scal, meta, t, acc, blocks):
    return call(
        functools.partial(later_body, fars), ACC,
        [SMEM, SMEM] + [VMEM] * (2 + len(fars)), VMEM,
        BLOCK_FLOPS * len(fars), aliases={3: 0}, name="later",
    )(scal, meta, t, acc, *blocks)


def further_call(scal, meta, base, t, acc, blocks):
    return call(
        further_body, ACC, [SMEM, SMEM, SMEM, VMEM, VMEM, VMEM], VMEM,
        BLOCK_FLOPS * REACH // 2, aliases={4: 0}, name="further",
    )(scal, meta, base, t, acc, blocks)


def shift(x, d):
    return lax.ppermute(x, "seq", [((i + d) % SHARDS, i) for i in range(SHARDS)])


def shift_z(x, d):
    return lax.ppermute(
        x, "seq", [(i // ROW * ROW + (i + d) % ROW, i) for i in range(SHARDS)]
    )


def body(
    queries, keys, values, out_grad, prefix_state, variant_queries, variant_grads,
    variant_owner, variant_position, doc_start,
):
    heads = queries.shape[1] // PAIR
    rows = queries.shape[0]
    scal = jnp.stack([lax.axis_index("seq").astype(I32), doc_start[0]])
    sent, msg = call(
        pack_body,
        (
            jax.ShapeDtypeStruct((heads, rows, 4 * PAIR), BF16),
            jax.ShapeDtypeStruct((16, 2 * PAIR), BF16),
        ),
        [VMEM] * 6 + [SMEM], (VMEM, VMEM), 1 << 20, name="pack",
    )(queries, out_grad, keys, values, variant_queries, variant_grads, scal)
    column = jnp.concatenate([msg] + [shift(msg, ROW * d) for d in range(1, COLS)], 0)
    t = lax.all_to_all(sent, "heads", split_axis=0, concat_axis=0).reshape(TOK, 4 * PAIR)
    across = [column] + [shift_z(column, d) for d in range(1, ROW)]
    own = t[:, 0 : 2 * PAIR]

    down, up = [shift(own, 1)], [shift(own, ROW)]
    for _ in range(3):
        down.append(shift(down[-1], 1))
        up.append(shift(up[-1], -1))

    acc = call(own_body, ACC, [SMEM, VMEM], VMEM, BLOCK_FLOPS * 3 // 2, name="own")(scal, t)
    acc = call(
        state_body, ACC, [SMEM, VMEM, VMEM, VMEM], VMEM, 3 * BLOCK_FLOPS,
        scratch=(
            pltpu.VMEM((4, FEAT, PAIR), F32),
            pltpu.VMEM((4, HEAD, PAIR), F32),
            pltpu.VMEM((4, HEAD, PAIR), F32),
            pltpu.VMEM((4, HEAD, PAIR), F32),
        ),
        aliases={3: 0}, name="state",
    )(scal, prefix_state[0], t, acc)
    acc, meta = call(
        variant_body, (ACC, jax.ShapeDtypeStruct((4,), I32)),
        [SMEM] + [VMEM] * (4 + ROW), (VMEM, SMEM), BLOCK_FLOPS,
        scratch=(pltpu.VMEM((TOK, 2 * PAIR), F32), pltpu.VMEM((SHARDS, 2 * PAIR), F32)),
        aliases={4: 0}, name="variant",
    )(scal, variant_owner.reshape(1, TOK), variant_position.reshape(1, TOK), t, acc, *across)
    for step in range(4):
        acc = later_call((step + 1, REACH - step), scal, meta, t, acc, (down[step], up[step]))

    def extend(acc):
        near = jnp.concatenate(down, 0)
        far = jnp.concatenate(up[::-1], 0)

        def go(carry):
            return carry[0] < meta[2]

        def more(carry):
            base, near, far, acc = carry
            moved = shift(near, REACH)
            acc = further_call(scal, meta, base.reshape(1), t, acc, moved)
            return base + REACH // 2, far, moved, acc

        return lax.while_loop(go, more, (jnp.int32(REACH), near, far, acc))[3]

    acc = lax.cond(meta[2] > REACH, extend, lambda a: a, acc)
    back = lax.all_to_all(acc.reshape(heads, rows, 3 * PAIR), "heads", split_axis=0, concat_axis=0)
    out = jax.ShapeDtypeStruct((rows, heads * PAIR), F32)
    return tuple(call(unpack_body, (out, out, out), [VMEM], (VMEM,) * 3, 1 << 20, name="unpack")(back))


def solution(mesh):
    tokens = P(("seq", "heads"), None)
    in_specs = (
        tokens, tokens, tokens, tokens, P("seq", None, "heads"), P("seq", "heads"),
        P("seq", "heads"), P(), P(), P("seq"),
    )
    return jax.shard_map(
        body, mesh=mesh, in_specs=in_specs, out_specs=(tokens,) * 3, check_vma=False
    )
```

```python
import functools
import math

import jax
import jax.numpy as jnp
from jax import lax
from jax.experimental import pallas as pl
from jax.experimental.pallas import tpu as pltpu
from jax.sharding import PartitionSpec as P

HEAD = 64
PAIR = 128
TOK = 256
FEAT = 2080
SHARDS = 32
ROW = 8
COLS = SHARDS // ROW
REACH = 11
F32 = jnp.float32
BF16 = jnp.bfloat16
I32 = jnp.int32

VMEM = pl.BlockSpec(memory_space=pltpu.VMEM)
SMEM = pl.BlockSpec(memory_space=pltpu.SMEM)


def call(body, out_shape, in_specs, out_specs, flops, scratch=(), aliases=None, name=None):
    return pl.pallas_call(
        body,
        out_shape=out_shape,
        in_specs=in_specs,
        out_specs=out_specs,
        scratch_shapes=list(scratch),
        input_output_aliases=aliases or {},
        compiler_params=pltpu.CompilerParams(vmem_limit_bytes=24 * 1024 * 1024),
        cost_estimate=pl.CostEstimate(flops=flops, bytes_accessed=1 << 20, transcendentals=0),
        name=name,
    )


def dot_nt(a, b):
    return lax.dot_general(a, b, (((1,), (1,)), ((), ())), preferred_element_type=F32)


def dot_tn(a, b):
    return lax.dot_general(a, b, (((0,), (0,)), ((), ())), preferred_element_type=F32)


def dot_nn(a, b):
    return lax.dot_general(a, b, (((1,), (0,)), ((), ())), preferred_element_type=F32)


def by_head(x):
    low = lax.broadcasted_iota(I32, x.shape, 1) < HEAD
    zero = jnp.zeros_like(x)
    return jnp.where(low, x, zero), jnp.where(low, zero, x)


def attend(q, g, keys, values, lo, hi):
    place = lax.broadcasted_iota(I32, (TOK, q.shape[0]), 0)
    seen = (place >= lo) & (place <= hi)
    slopes, squares = [], []
    for k, v in zip(by_head(keys), by_head(values)):
        score = jnp.where(seen, dot_nt(k, q), 0.0)
        inner = dot_nt(v, g)
        slopes.append((2.0 * score * inner).astype(BF16))
        squares.append((score * score).astype(BF16))
    slope = jnp.concatenate(slopes, 1)
    square = jnp.concatenate(squares, 1)
    k_part = dot_nn(slope, jnp.concatenate(by_head(q), 0))
    v_part = dot_nn(square, jnp.concatenate(by_head(g), 0))
    return slopes, k_part, v_part


def pack_body(start, q, g, k, v, vq, vg, out, msg, buf, sems):
    copies = [
        pltpu.make_async_copy(ref, buf.at[n], sems.at[n]) for n, ref in enumerate((q, g, k, v))
    ]
    for copy in copies:
        copy.start()
    top = jnp.concatenate([vq[...], vg[...]], 1).astype(F32)
    low = jnp.full((8, 2 * PAIR), start[0].astype(F32))
    msg[...] = jnp.concatenate([top, low], 0).astype(BF16)
    for n, copy in enumerate(copies):
        copy.wait()
        for h in range(out.shape[0]):
            out[h, :, n * PAIR : (n + 1) * PAIR] = buf[n, :, h * PAIR : (h + 1) * PAIR]


def unpack_body(x, qo, ko, vo):
    for h in range(x.shape[0]):
        for n, ref in enumerate((qo, ko, vo)):
            ref[:, h * PAIR : (h + 1) * PAIR] = x[h, :, n * PAIR : (n + 1) * PAIR]


def assemble_body(t, *rest):
    msgs, (block, rows) = rest[:COLS], rest[COLS:]
    x = lax.div(lax.axis_index("seq"), ROW)
    block[0:TOK, :] = t[:, 0 : 2 * PAIR]
    group = lax.shift_right_logical(lax.broadcasted_iota(I32, (16, 2 * PAIR), 0), 2)
    starts = jnp.zeros((16, 2 * PAIR), F32)
    for dx, msg in enumerate(msgs):
        at = lax.rem(x + dx, COLS)
        piece = msg[...].astype(F32)
        rows[pl.ds(pl.multiple_of(at * 8, 8), 8), :] = piece[0:8, :]
        starts = jnp.where(group == at, piece[8:9, :], starts)
    block[TOK : TOK + 32, :] = rows[...].astype(BF16)
    block[TOK + 32 : TOK + 48, :] = starts.astype(BF16)


def own_body(start_ref, t, acc):
    start = start_ref[0]
    spot = lax.broadcasted_iota(I32, (1, TOK), 1)
    lo = jnp.where(spot >= start, start, 0)
    q, g, k, v = (t[:, n * PAIR : (n + 1) * PAIR] for n in range(4))
    slopes, k_part, v_part = attend(q, g, k, v, lo, spot)
    k0, k1 = by_head(k)
    acc[:, 0:PAIR] = dot_tn(slopes[0], k0) + dot_tn(slopes[1], k1)
    acc[:, PAIR : 2 * PAIR] = k_part
    acc[:, 2 * PAIR : 3 * PAIR] = v_part


def state_body(start_ref, m, t, acc_in, acc, pt, qt, rows, res):
    start = start_ref[0]
    chunk = 416
    for h, g in enumerate(by_head(t[:, PAIR : 2 * PAIR])):
        for c in range(0, FEAT, chunk):
            r = dot_nt(m[c : c + chunk, :], g)
            pt[2 * h, c : c + chunk, :] = r[:, 0:PAIR]
            pt[2 * h + 1, c : c + chunk, :] = r[:, PAIR : 2 * PAIR]
    q_t = t[:, 0:PAIR].astype(F32).T
    for h in range(2):
        for half in range(2):
            qt[2 * h + half] = q_t[h * HEAD : (h + 1) * HEAD, half * PAIR : (half + 1) * PAIR]
    sub = lax.broadcasted_iota(I32, (8, PAIR), 0)

    def part(i, carry):
        tiles = HEAD // 8
        sums = [jnp.zeros((8, PAIR), F32) for _ in range(tiles)]
        for a in range(HEAD):
            first = a // 8
            at = a * HEAD - a * (a - 1) // 2 - a % 8
            qa = qt[i, a : a + 1, :]
            row = None
            for b in range(first, tiles):
                tile = pt[i, at + 8 * (b - first) : at + 8 * (b - first) + 8, :]
                if b == first:
                    scale = jnp.where(sub > a % 8, 1.0, jnp.where(sub == a % 8, math.sqrt(0.5), 0.0))
                    tile = tile * scale
                sums[b] = sums[b] + tile * qa
                more = tile * qt[i, 8 * b : 8 * b + 8, :]
                row = more if row is None else row + more
            rows[i, a : a + 1, :] = jnp.sum(row, axis=0, keepdims=True)
        for b in range(tiles):
            res[i, 8 * b : 8 * b + 8, :] = math.sqrt(2.0) * (sums[b] + rows[i, 8 * b : 8 * b + 8, :])
        return carry

    lax.fori_loop(0, 4, part, 0)
    for half in range(2):
        both = jnp.concatenate([res[half], res[2 + half]], 0).T
        spot = half * PAIR + lax.broadcasted_iota(I32, (PAIR, PAIR), 0)
        at = slice(half * PAIR, (half + 1) * PAIR)
        acc[at, 0:PAIR] = acc_in[at, 0:PAIR] + jnp.where(spot < start, both, 0.0)
    acc[:, PAIR : 3 * PAIR] = acc_in[:, PAIR : 3 * PAIR]


def later_part(far, start, t, block):
    x = lax.rem(lax.div(lax.axis_index("seq") + far, ROW), COLS)
    group = lax.shift_right_logical(lax.broadcasted_iota(I32, (16, 2 * PAIR), 0), 2)
    begin = block[TOK + 32 : TOK + 48, :].astype(F32)
    until = jnp.max(jnp.where(group == x, begin, 0.0), axis=0, keepdims=True).astype(I32)
    spot = lax.broadcasted_iota(I32, (1, TOK), 1)
    lo = jnp.where(start == TOK, 0, start)
    hi = jnp.where(spot < until, TOK - 1, -1)
    k, v = t[:, 2 * PAIR : 3 * PAIR], t[:, 3 * PAIR : 4 * PAIR]
    q, g = block[0:TOK, 0:PAIR], block[0:TOK, PAIR : 2 * PAIR]
    _, k_part, v_part = attend(q, g, k, v, lo, hi)
    return k_part, v_part


def later_body(fars, start_ref, t, *rest):
    blocks, out = rest[:-1], rest[-1]
    for n, (far, block) in enumerate(zip(fars, blocks)):
        k_part, v_part = later_part(far, start_ref[0], t, block)
        out[n, :, 0:PAIR] = k_part
        out[n, :, PAIR : 2 * PAIR] = v_part


def add_later(far, count, start, t, block, acc):
    @pl.when(far <= count)
    def _():
        k_part, v_part = later_part(far, start, t, block)
        acc[:, PAIR : 2 * PAIR] += k_part
        acc[:, 2 * PAIR : 3 * PAIR] += v_part


def final_body(done, rest_fars, start_ref, owner_ref, place_ref, t, acc_in, *refs):
    refs = list(refs)
    columns = [refs.pop(0) for _ in range(ROW)]
    parts = [refs.pop(0) for _ in done]
    blocks = [refs.pop(0) for _ in rest_fars]
    acc, longest, count, rows, starts = refs
    shard = lax.axis_index("seq")
    start = start_ref[0]
    z = lax.rem(shard, ROW)
    for block, dz in zip(columns, (0, 1, 2, 3, 4, 7, 6, 5)):
        piece = block[TOK : TOK + 48, :].astype(F32)
        zz = lax.rem(z + dz, ROW)
        for x in range(COLS):
            at = x * ROW + zz
            rows[pl.ds(pl.multiple_of(at * 8, 8), 8), :] = piece[8 * x : 8 * x + 8, :]
            starts[pl.ds(at, 1), :] = piece[32 + 4 * x : 33 + 4 * x, :]
    begin = starts[...]
    sub = lax.broadcasted_iota(I32, (SHARDS, TOK), 0)
    lane = lax.broadcasted_iota(I32, (SHARDS, TOK), 1)
    along = jnp.sum(jnp.where(sub == lane, begin, 0.0), axis=0, keepdims=True)
    stops = (lane > sub) & (lane < SHARDS) & (along < TOK)
    last = jnp.min(jnp.where(stops, lane, SHARDS - 1).astype(F32), axis=1, keepdims=True)
    sub1 = lax.broadcasted_iota(I32, (SHARDS, 1), 0)
    longest[0] = jnp.max(last - sub1.astype(F32)).astype(I32)
    mine = jnp.sum(jnp.where(sub1 == shard, last, 0.0)).astype(I32)
    reach = mine - shard
    count[0] = reach
    owner = owner_ref[...]
    place = place_ref[...]
    theirs = jnp.sum(jnp.where(sub == owner, begin, 0.0), axis=0, keepdims=True).astype(I32)
    here = owner == shard
    after = (owner > shard) & (owner <= mine) & (place < theirs)
    carry_lo = jnp.where(start == TOK, 0, start)
    lo = jnp.where(here, jnp.where(place >= start, start, 0), carry_lo)
    hi = jnp.where(here, place, jnp.where(after, TOK - 1, -1))
    both = rows[...].astype(BF16)
    k, v = t[:, 2 * PAIR : 3 * PAIR], t[:, 3 * PAIR : 4 * PAIR]
    _, k_part, v_part = attend(both[:, 0:PAIR], both[:, PAIR:], k, v, lo, hi)
    acc[:, 0:PAIR] = acc_in[:, 0:PAIR]
    acc[:, PAIR : 2 * PAIR] = acc_in[:, PAIR : 2 * PAIR] + k_part
    acc[:, 2 * PAIR : 3 * PAIR] = acc_in[:, 2 * PAIR : 3 * PAIR] + v_part
    for fars, part in zip(done, parts):
        for n, far in enumerate(fars):

            @pl.when(far <= reach)
            def _():
                acc[:, PAIR : 3 * PAIR] += part[n]

    for far, block in zip(rest_fars, blocks):
        add_later(far, reach, start, t, block, acc)


def further_body(start_ref, count, base, t, acc_in, *rest):
    blocks, acc = rest[:-1], rest[-1]
    acc[...] = acc_in[...]
    for n, block in enumerate(blocks):
        add_later(base[0] + n + 1, count[0], start_ref[0], t, block, acc)


ACC = jax.ShapeDtypeStruct((TOK, 3 * PAIR), F32)
BLOCK = jax.ShapeDtypeStruct((TOK + 48, 2 * PAIR), BF16)
BLOCK_FLOPS = 8 * 2 * TOK * TOK * PAIR


def later_call(fars, start, t, blocks):
    return call(
        functools.partial(later_body, fars),
        jax.ShapeDtypeStruct((len(fars), TOK, 2 * PAIR), F32),
        [SMEM] + [VMEM] * (1 + len(fars)), VMEM, BLOCK_FLOPS * len(fars), name="later",
    )(start, t, *blocks)


def further_call(start, count, base, t, acc, blocks):
    return call(
        further_body, ACC, [SMEM, SMEM, SMEM] + [VMEM] * (2 + len(blocks)), VMEM,
        BLOCK_FLOPS * len(blocks), aliases={4: 0}, name="further",
    )(start, count, base, t, acc, *blocks)


def shift(x, d):
    return lax.ppermute(x, "seq", [((i + d) % SHARDS, i) for i in range(SHARDS)])


def body(
    queries, keys, values, out_grad, prefix_state, variant_queries, variant_grads,
    variant_owner, variant_position, start,
):
    heads = queries.shape[1] // PAIR
    rows = queries.shape[0]
    anywhere = pl.BlockSpec(memory_space=pl.ANY)
    sent, msg = call(
        pack_body,
        (
            jax.ShapeDtypeStruct((heads, rows, 4 * PAIR), BF16),
            jax.ShapeDtypeStruct((16, 2 * PAIR), BF16),
        ),
        [SMEM] + [anywhere] * 4 + [VMEM] * 2, (VMEM, VMEM), 1 << 20,
        scratch=(pltpu.VMEM((4, rows, heads * PAIR), BF16), pltpu.SemaphoreType.DMA((4,))),
        name="pack",
    )(start, queries, out_grad, keys, values, variant_queries, variant_grads)
    msgs = [msg] + [shift(msg, ROW * d) for d in range(1, COLS)]
    t = lax.all_to_all(sent, "heads", split_axis=0, concat_axis=0).reshape(TOK, 4 * PAIR)
    own = call(
        assemble_body, BLOCK, [VMEM] * (1 + COLS), VMEM, 1 << 20,
        scratch=(pltpu.VMEM((32, 2 * PAIR), F32),), name="assemble",
    )(t, *msgs)

    down, up, over = [shift(own, 1)], [shift(own, ROW)], []
    for _ in range(3):
        over.append(shift(down[-1], ROW))
        down.append(shift(down[-1], 1))
        up.append(shift(up[-1], -1))
    blocks = dict(zip(range(1, 5), down)) | dict(zip((8, 7, 6, 5), up)) | dict(zip((9, 10, 11), over))

    acc = call(own_body, ACC, [SMEM, VMEM], VMEM, BLOCK_FLOPS * 3 // 2, name="own")(start, t)
    acc = call(
        state_body, ACC, [SMEM, VMEM, VMEM, VMEM], VMEM, 3 * BLOCK_FLOPS,
        scratch=(
            pltpu.VMEM((4, FEAT, PAIR), F32),
            pltpu.VMEM((4, HEAD, PAIR), F32),
            pltpu.VMEM((4, HEAD, PAIR), F32),
            pltpu.VMEM((4, HEAD, PAIR), F32),
        ),
        aliases={3: 0}, name="state",
    )(start, prefix_state[0], t, acc)
    done = ((1, 8), (2, 7), (3, 6, 9))
    parts = [later_call(fars, start, t, [blocks[far] for far in fars]) for fars in done]
    left = (4, 5, 10, 11)
    one = jax.ShapeDtypeStruct((1,), I32)
    columns = [own] + down + up[1:]
    acc, longest, count = call(
        functools.partial(final_body, done, left), (ACC, one, one),
        [SMEM] + [VMEM] * (4 + ROW + len(done) + len(left)), (VMEM, SMEM, SMEM), BLOCK_FLOPS,
        scratch=(pltpu.VMEM((TOK, 2 * PAIR), F32), pltpu.VMEM((SHARDS, 2 * PAIR), F32)),
        aliases={4: 0}, name="final",
    )(
        start, variant_owner.reshape(1, TOK), variant_position.reshape(1, TOK), t, acc,
        *columns, *parts, *[blocks[far] for far in left],
    )
    longest = longest.reshape(())

    def extend(acc):
        def go(carry):
            return carry[0] < longest

        def more(carry):
            base, near, far, acc = carry
            moved = [shift(block, ROW) for block in near]
            acc = further_call(start, count, base.reshape(1), t, acc, moved)
            return base + len(near), far, moved, acc

        near = [blocks[n] for n in (4, 5, 6, 7)]
        far = [blocks[n] for n in (8, 9, 10, 11)]
        return lax.while_loop(go, more, (jnp.int32(REACH), near, far, acc))[3]

    acc = lax.cond(longest > REACH, extend, lambda a: a, acc)
    back = lax.all_to_all(acc.reshape(heads, rows, 3 * PAIR), "heads", split_axis=0, concat_axis=0)
    out = jax.ShapeDtypeStruct((rows, heads * PAIR), F32)
    return tuple(call(unpack_body, (out, out, out), [VMEM], (VMEM,) * 3, 1 << 20, name="unpack")(back))


def solution(mesh):
    tokens = P(("seq", "heads"), None)
    in_specs = (
        tokens, tokens, tokens, tokens, P("seq", None, "heads"), P("seq", "heads"),
        P("seq", "heads"), P(), P(), P("seq"),
    )
    return jax.shard_map(
        body, mesh=mesh, in_specs=in_specs, out_specs=(tokens,) * 3, check_vma=False
    )
```

```python
import functools
import math

import jax
import jax.numpy as jnp
from jax import lax
from jax.experimental import pallas as pl
from jax.experimental.pallas import tpu as pltpu
from jax.sharding import PartitionSpec as P

HEAD = 64
PAIR = 128
TOK = 256
FEAT = 2080
SHARDS = 32
ROW = 8
COLS = SHARDS // ROW
REACH = 10
F32 = jnp.float32
BF16 = jnp.bfloat16
I32 = jnp.int32

VMEM = pl.BlockSpec(memory_space=pltpu.VMEM)
SMEM = pl.BlockSpec(memory_space=pltpu.SMEM)


def call(body, out_shape, in_specs, out_specs, flops, scratch=(), aliases=None, name=None,
         vmem=24):
    return pl.pallas_call(
        body,
        out_shape=out_shape,
        in_specs=in_specs,
        out_specs=out_specs,
        scratch_shapes=list(scratch),
        input_output_aliases=aliases or {},
        compiler_params=pltpu.CompilerParams(vmem_limit_bytes=vmem * 1024 * 1024),
        cost_estimate=pl.CostEstimate(flops=flops, bytes_accessed=1 << 20, transcendentals=0),
        name=name,
    )


def dot_nt(a, b):
    return lax.dot_general(a, b, (((1,), (1,)), ((), ())), preferred_element_type=F32)


def dot_tn(a, b):
    return lax.dot_general(a, b, (((0,), (0,)), ((), ())), preferred_element_type=F32)


def dot_nn(a, b):
    return lax.dot_general(a, b, (((1,), (0,)), ((), ())), preferred_element_type=F32)


def by_head(x):
    low = lax.broadcasted_iota(I32, x.shape, 1) < HEAD
    zero = jnp.zeros_like(x)
    return jnp.where(low, x, zero), jnp.where(low, zero, x)


def attend(q, g, keys, values, lo, hi):
    place = lax.broadcasted_iota(I32, (TOK, q.shape[0]), 0)
    seen = (place >= lo) & (place <= hi)
    slopes, squares = [], []
    for k, v in zip(by_head(keys), by_head(values)):
        score = jnp.where(seen, dot_nt(k, q), 0.0)
        inner = dot_nt(v, g)
        slopes.append((2.0 * score * inner).astype(BF16))
        squares.append((score * score).astype(BF16))
    slope = jnp.concatenate(slopes, 1)
    square = jnp.concatenate(squares, 1)
    k_part = dot_nn(slope, jnp.concatenate(by_head(q), 0))
    v_part = dot_nn(square, jnp.concatenate(by_head(g), 0))
    return slopes, k_part, v_part


def pack_body(start, q, g, k, v, vq, vg, out, msg, buf, sems):
    copies = [
        pltpu.make_async_copy(ref, buf.at[n], sems.at[n]) for n, ref in enumerate((q, g, k, v))
    ]
    for copy in copies:
        copy.start()
    top = jnp.concatenate([vq[...], vg[...]], 1).astype(F32)
    low = jnp.full((8, 2 * PAIR), start[0].astype(F32))
    msg[...] = jnp.concatenate([top, low], 0).astype(BF16)
    for n, copy in enumerate(copies):
        copy.wait()
        for h in range(out.shape[0]):
            out[h, :, n * PAIR : (n + 1) * PAIR] = buf[n, :, h * PAIR : (h + 1) * PAIR]


def unpack_body(x, qo, ko, vo):
    for h in range(x.shape[0]):
        for n, ref in enumerate((qo, ko, vo)):
            ref[:, h * PAIR : (h + 1) * PAIR] = x[h, :, n * PAIR : (n + 1) * PAIR]


def assemble_body(t, *rest):
    msgs, (block, rows) = rest[:COLS], rest[COLS:]
    x = lax.div(lax.axis_index("seq"), ROW)
    block[0:TOK, :] = t[:, 0 : 2 * PAIR]
    group = lax.shift_right_logical(lax.broadcasted_iota(I32, (16, 2 * PAIR), 0), 2)
    starts = jnp.zeros((16, 2 * PAIR), F32)
    for dx, msg in enumerate(msgs):
        at = lax.rem(x + dx, COLS)
        piece = msg[...].astype(F32)
        rows[pl.ds(pl.multiple_of(at * 8, 8), 8), :] = piece[0:8, :]
        starts = jnp.where(group == at, piece[8:9, :], starts)
    block[TOK : TOK + 32, :] = rows[...].astype(BF16)
    block[TOK + 32 : TOK + 48, :] = starts.astype(BF16)


def own_body(start_ref, t, acc):
    start = start_ref[0]
    spot = lax.broadcasted_iota(I32, (1, TOK), 1)
    lo = jnp.where(spot >= start, start, 0)
    q, g, k, v = (t[:, n * PAIR : (n + 1) * PAIR] for n in range(4))
    slopes, k_part, v_part = attend(q, g, k, v, lo, spot)
    k0, k1 = by_head(k)
    acc[:, 0:PAIR] = dot_tn(slopes[0], k0) + dot_tn(slopes[1], k1)
    acc[:, PAIR : 2 * PAIR] = k_part
    acc[:, 2 * PAIR : 3 * PAIR] = v_part


def state_body(start_ref, m, t, acc_in, acc, pt, qt, rows, res):
    start = start_ref[0]
    chunk = 416
    for h, g in enumerate(by_head(t[:, PAIR : 2 * PAIR])):
        for c in range(0, FEAT, chunk):
            r = dot_nt(m[c : c + chunk, :], g)
            pt[2 * h, c : c + chunk, :] = r[:, 0:PAIR]
            pt[2 * h + 1, c : c + chunk, :] = r[:, PAIR : 2 * PAIR]
    q_t = t[:, 0:PAIR].astype(F32).T
    for h in range(2):
        for half in range(2):
            qt[2 * h + half] = q_t[h * HEAD : (h + 1) * HEAD, half * PAIR : (half + 1) * PAIR]
    sub = lax.broadcasted_iota(I32, (8, PAIR), 0)

    def part(i, carry):
        tiles = HEAD // 8
        sums = [jnp.zeros((8, PAIR), F32) for _ in range(tiles)]
        for a in range(HEAD):
            first = a // 8
            at = a * HEAD - a * (a - 1) // 2 - a % 8
            qa = qt[i, a : a + 1, :]
            row = None
            for b in range(first, tiles):
                tile = pt[i, at + 8 * (b - first) : at + 8 * (b - first) + 8, :]
                if b == first:
                    scale = jnp.where(sub > a % 8, 1.0, jnp.where(sub == a % 8, math.sqrt(0.5), 0.0))
                    tile = tile * scale
                sums[b] = sums[b] + tile * qa
                more = tile * qt[i, 8 * b : 8 * b + 8, :]
                row = more if row is None else row + more
            rows[i, a : a + 1, :] = jnp.sum(row, axis=0, keepdims=True)
        for b in range(tiles):
            res[i, 8 * b : 8 * b + 8, :] = math.sqrt(2.0) * (sums[b] + rows[i, 8 * b : 8 * b + 8, :])
        return carry

    lax.fori_loop(0, 4, part, 0)
    for half in range(2):
        both = jnp.concatenate([res[half], res[2 + half]], 0).T
        spot = half * PAIR + lax.broadcasted_iota(I32, (PAIR, PAIR), 0)
        at = slice(half * PAIR, (half + 1) * PAIR)
        acc[at, 0:PAIR] = acc_in[at, 0:PAIR] + jnp.where(spot < start, both, 0.0)
    acc[:, PAIR : 3 * PAIR] = acc_in[:, PAIR : 3 * PAIR]


def later_part(far, start, t, block):
    x = lax.rem(lax.div(lax.axis_index("seq") + far, ROW), COLS)
    group = lax.shift_right_logical(lax.broadcasted_iota(I32, (16, 2 * PAIR), 0), 2)
    begin = block[TOK + 32 : TOK + 48, :].astype(F32)
    until = jnp.max(jnp.where(group == x, begin, 0.0), axis=0, keepdims=True).astype(I32)
    spot = lax.broadcasted_iota(I32, (1, TOK), 1)
    lo = jnp.where(start == TOK, 0, start)
    hi = jnp.where(spot < until, TOK - 1, -1)
    k, v = t[:, 2 * PAIR : 3 * PAIR], t[:, 3 * PAIR : 4 * PAIR]
    q, g = block[0:TOK, 0:PAIR], block[0:TOK, PAIR : 2 * PAIR]
    _, k_part, v_part = attend(q, g, k, v, lo, hi)
    return k_part, v_part


def later_body(fars, start_ref, t, *rest):
    blocks, out = rest[:-1], rest[-1]
    for n, (far, block) in enumerate(zip(fars, blocks)):
        k_part, v_part = later_part(far, start_ref[0], t, block)
        out[n, :, 0:PAIR] = k_part
        out[n, :, PAIR : 2 * PAIR] = v_part


def add_later(far, count, start, t, block, acc):
    @pl.when(far <= count)
    def _():
        k_part, v_part = later_part(far, start, t, block)
        acc[:, PAIR : 2 * PAIR] += k_part
        acc[:, 2 * PAIR : 3 * PAIR] += v_part


def final_body(done, rest_fars, start_ref, owner_ref, place_ref, t, acc_in, *refs):
    refs = list(refs)
    columns = [refs.pop(0) for _ in range(ROW)]
    parts = [refs.pop(0) for _ in done]
    blocks = [refs.pop(0) for _ in rest_fars]
    acc, longest, count, rows, starts = refs
    shard = lax.axis_index("seq")
    start = start_ref[0]
    z = lax.rem(shard, ROW)
    for block, dz in zip(columns, range(ROW)):
        piece = block[TOK : TOK + 48, :].astype(F32)
        zz = lax.rem(z + dz, ROW)
        for x in range(COLS):
            at = x * ROW + zz
            rows[pl.ds(pl.multiple_of(at * 8, 8), 8), :] = piece[8 * x : 8 * x + 8, :]
            starts[pl.ds(at, 1), :] = piece[32 + 4 * x : 33 + 4 * x, :]
    begin = starts[...]
    sub = lax.broadcasted_iota(I32, (SHARDS, TOK), 0)
    lane = lax.broadcasted_iota(I32, (SHARDS, TOK), 1)
    along = jnp.sum(jnp.where(sub == lane, begin, 0.0), axis=0, keepdims=True)
    stops = (lane > sub) & (lane < SHARDS) & (along < TOK)
    last = jnp.min(jnp.where(stops, lane, SHARDS - 1).astype(F32), axis=1, keepdims=True)
    sub1 = lax.broadcasted_iota(I32, (SHARDS, 1), 0)
    longest[0] = jnp.max(last - sub1.astype(F32)).astype(I32)
    mine = jnp.sum(jnp.where(sub1 == shard, last, 0.0)).astype(I32)
    reach = mine - shard
    count[0] = reach
    owner = owner_ref[...]
    place = place_ref[...]
    theirs = jnp.sum(jnp.where(sub == owner, begin, 0.0), axis=0, keepdims=True).astype(I32)
    here = owner == shard
    after = (owner > shard) & (owner <= mine) & (place < theirs)
    carry_lo = jnp.where(start == TOK, 0, start)
    lo = jnp.where(here, jnp.where(place >= start, start, 0), carry_lo)
    hi = jnp.where(here, place, jnp.where(after, TOK - 1, -1))
    both = rows[...].astype(BF16)
    k, v = t[:, 2 * PAIR : 3 * PAIR], t[:, 3 * PAIR : 4 * PAIR]
    _, k_part, v_part = attend(both[:, 0:PAIR], both[:, PAIR:], k, v, lo, hi)
    acc[:, 0:PAIR] = acc_in[:, 0:PAIR]
    acc[:, PAIR : 2 * PAIR] = acc_in[:, PAIR : 2 * PAIR] + k_part
    acc[:, 2 * PAIR : 3 * PAIR] = acc_in[:, 2 * PAIR : 3 * PAIR] + v_part
    for fars, part in zip(done, parts):
        for n, far in enumerate(fars):

            @pl.when(far <= reach)
            def _():
                acc[:, PAIR : 3 * PAIR] += part[n]

    for far, block in zip(rest_fars, blocks):
        add_later(far, reach, start, t, block, acc)


def further_body(start_ref, count, base, t, acc_in, *rest):
    blocks, acc = rest[:-1], rest[-1]
    acc[...] = acc_in[...]
    for n, block in enumerate(blocks):
        add_later(base[0] + n + 1, count[0], start_ref[0], t, block, acc)


ACC = jax.ShapeDtypeStruct((TOK, 3 * PAIR), F32)
BLOCK = jax.ShapeDtypeStruct((TOK + 48, 2 * PAIR), BF16)
BLOCK_FLOPS = 8 * 2 * TOK * TOK * PAIR


def later_call(fars, start, t, blocks):
    return call(
        functools.partial(later_body, fars),
        jax.ShapeDtypeStruct((len(fars), TOK, 2 * PAIR), F32),
        [SMEM] + [VMEM] * (1 + len(fars)), VMEM, BLOCK_FLOPS * len(fars), name="later",
    )(start, t, *blocks)


def further_call(start, count, base, t, acc, blocks):
    return call(
        further_body, ACC, [SMEM, SMEM, SMEM] + [VMEM] * (2 + len(blocks)), VMEM,
        BLOCK_FLOPS * len(blocks), aliases={4: 0}, name="further",
    )(start, count, base, t, acc, *blocks)


def shift(x, d):
    return lax.ppermute(x, "seq", [((i + d) % SHARDS, i) for i in range(SHARDS)])


def body(
    queries, keys, values, out_grad, prefix_state, variant_queries, variant_grads,
    variant_owner, variant_position, start,
):
    heads = queries.shape[1] // PAIR
    rows = queries.shape[0]
    anywhere = pl.BlockSpec(memory_space=pltpu.HBM)
    sent, msg = call(
        pack_body,
        (
            jax.ShapeDtypeStruct((heads, rows, 4 * PAIR), BF16),
            jax.ShapeDtypeStruct((16, 2 * PAIR), BF16),
        ),
        [SMEM] + [anywhere] * 4 + [VMEM] * 2, (VMEM, VMEM), 1 << 20,
        scratch=(pltpu.VMEM((4, rows, heads * PAIR), BF16), pltpu.SemaphoreType.DMA((4,))),
        name="pack", vmem=60,
    )(start, queries, out_grad, keys, values, variant_queries, variant_grads)
    msgs = [msg] + [shift(msg, ROW * d) for d in range(1, COLS)]
    t = lax.all_to_all(sent, "heads", split_axis=0, concat_axis=0).reshape(TOK, 4 * PAIR)
    own = call(
        assemble_body, BLOCK, [VMEM] * (1 + COLS), VMEM, 1 << 20,
        scratch=(pltpu.VMEM((32, 2 * PAIR), F32),), name="assemble",
    )(t, *msgs)

    blocks = {far: shift(own, far) for far in (1, 2, 7, 8)}
    acc = call(own_body, ACC, [SMEM, VMEM], VMEM, BLOCK_FLOPS * 3 // 2, name="own")(start, t)
    acc = call(
        state_body, ACC, [SMEM, VMEM, VMEM, VMEM], VMEM, 3 * BLOCK_FLOPS,
        scratch=(
            pltpu.VMEM((4, FEAT, PAIR), F32),
            pltpu.VMEM((4, HEAD, PAIR), F32),
            pltpu.VMEM((4, HEAD, PAIR), F32),
            pltpu.VMEM((4, HEAD, PAIR), F32),
        ),
        aliases={3: 0}, name="state",
    )(start, prefix_state[0], t, acc)
    blocks, acc = lax.optimization_barrier((blocks, acc))
    for far, via in ((3, 2), (6, 7), (4, 2), (5, 7), (9, 1), (10, 2)):
        blocks[far] = shift(blocks[via], far - via)
    done = ((1, 8), (2, 7))
    parts = [later_call(fars, start, t, [blocks[far] for far in fars]) for fars in done]
    left = (3, 4, 5, 6, 9, 10)
    one = jax.ShapeDtypeStruct((1,), I32)
    columns = [own] + [blocks[far] for far in range(1, ROW)]
    acc, longest, count = call(
        functools.partial(final_body, done, left), (ACC, one, one),
        [SMEM] + [VMEM] * (4 + ROW + len(done) + len(left)), (VMEM, SMEM, SMEM), BLOCK_FLOPS,
        scratch=(pltpu.VMEM((TOK, 2 * PAIR), F32), pltpu.VMEM((SHARDS, 2 * PAIR), F32)),
        aliases={4: 0}, name="final",
    )(
        start, variant_owner.reshape(1, TOK), variant_position.reshape(1, TOK), t, acc,
        *columns, *parts, *[blocks[far] for far in left],
    )
    longest = longest.reshape(())

    def extend(acc):
        def go(carry):
            return carry[0] < longest

        def more(carry):
            base, near, far, acc = carry
            moved = [shift(block, ROW) for block in near]
            acc = further_call(start, count, base.reshape(1), t, acc, moved)
            return base + len(near), far, moved, acc

        near = [blocks[n] for n in (3, 4, 5, 6)]
        far = [blocks[n] for n in (7, 8, 9, 10)]
        return lax.while_loop(go, more, (jnp.int32(REACH), near, far, acc))[3]

    acc = lax.cond(longest > REACH, extend, lambda a: a, acc)
    back = lax.all_to_all(acc.reshape(heads, rows, 3 * PAIR), "heads", split_axis=0, concat_axis=0)
    out = jax.ShapeDtypeStruct((rows, heads * PAIR), F32)
    return tuple(call(unpack_body, (out, out, out), [VMEM], (VMEM,) * 3, 1 << 20, name="unpack")(back))


def solution(mesh):
    tokens = P(("seq", "heads"), None)
    in_specs = (
        tokens, tokens, tokens, tokens, P("seq", None, "heads"), P("seq", "heads"),
        P("seq", "heads"), P(), P(), P("seq"),
    )
    return jax.shard_map(
        body, mesh=mesh, in_specs=in_specs, out_specs=(tokens,) * 3, check_vma=False
    )
```

```python
import functools
import math

import jax
import jax.numpy as jnp
from jax import lax
from jax.experimental import pallas as pl
from jax.experimental.pallas import tpu as pltpu
from jax.sharding import PartitionSpec as P

HEAD = 64
PAIR = 128
TOK = 256
FEAT = 2080
SHARDS = 32
ROW = 8
COLS = SHARDS // ROW
REACH = 10
F32 = jnp.float32
BF16 = jnp.bfloat16
I32 = jnp.int32

VMEM = pl.BlockSpec(memory_space=pltpu.VMEM)
SMEM = pl.BlockSpec(memory_space=pltpu.SMEM)


def call(body, out_shape, in_specs, out_specs, flops, scratch=(), aliases=None, name=None,
         vmem=24):
    return pl.pallas_call(
        body,
        out_shape=out_shape,
        in_specs=in_specs,
        out_specs=out_specs,
        scratch_shapes=list(scratch),
        input_output_aliases=aliases or {},
        compiler_params=pltpu.CompilerParams(vmem_limit_bytes=vmem * 1024 * 1024),
        cost_estimate=pl.CostEstimate(flops=flops, bytes_accessed=1 << 20, transcendentals=0),
        name=name,
    )


def dot_nt(a, b):
    return lax.dot_general(a, b, (((1,), (1,)), ((), ())), preferred_element_type=F32)


def dot_tn(a, b):
    return lax.dot_general(a, b, (((0,), (0,)), ((), ())), preferred_element_type=F32)


def dot_nn(a, b):
    return lax.dot_general(a, b, (((1,), (0,)), ((), ())), preferred_element_type=F32)


def by_head(x):
    low = lax.broadcasted_iota(I32, x.shape, 1) < HEAD
    zero = jnp.zeros_like(x)
    return jnp.where(low, x, zero), jnp.where(low, zero, x)


def attend(q, g, keys, values, lo, hi):
    place = lax.broadcasted_iota(I32, (TOK, q.shape[0]), 0)
    seen = (place >= lo) & (place <= hi)
    slopes, squares = [], []
    for k, v in zip(by_head(keys), by_head(values)):
        score = jnp.where(seen, dot_nt(k, q), 0.0)
        inner = dot_nt(v, g)
        slopes.append((2.0 * score * inner).astype(BF16))
        squares.append((score * score).astype(BF16))
    slope = jnp.concatenate(slopes, 1)
    square = jnp.concatenate(squares, 1)
    k_part = dot_nn(slope, jnp.concatenate(by_head(q), 0))
    v_part = dot_nn(square, jnp.concatenate(by_head(g), 0))
    return slopes, k_part, v_part


def pack_body(start, q, g, k, v, vq, vg, out, msg, buf, sems):
    copies = [
        pltpu.make_async_copy(ref, buf.at[n], sems.at[n]) for n, ref in enumerate((q, g, k, v))
    ]
    for copy in copies:
        copy.start()
    top = jnp.concatenate([vq[...], vg[...]], 1).astype(F32)
    low = jnp.full((8, 2 * PAIR), start[0].astype(F32))
    msg[...] = jnp.concatenate([top, low], 0).astype(BF16)
    for n, copy in enumerate(copies):
        copy.wait()
        for h in range(out.shape[0]):
            out[h, :, n * PAIR : (n + 1) * PAIR] = buf[n, :, h * PAIR : (h + 1) * PAIR]


def unpack_body(x, qo, ko, vo):
    for h in range(x.shape[0]):
        for n, ref in enumerate((qo, ko, vo)):
            ref[:, h * PAIR : (h + 1) * PAIR] = x[h, :, n * PAIR : (n + 1) * PAIR]


def assemble_body(t, *rest):
    msgs, (block, rows) = rest[:COLS], rest[COLS:]
    x = lax.div(lax.axis_index("seq"), ROW)
    block[0:TOK, :] = t[:, 0 : 2 * PAIR]
    group = lax.shift_right_logical(lax.broadcasted_iota(I32, (16, 2 * PAIR), 0), 2)
    starts = jnp.zeros((16, 2 * PAIR), F32)
    for dx, msg in enumerate(msgs):
        at = lax.rem(x + dx, COLS)
        piece = msg[...].astype(F32)
        rows[pl.ds(pl.multiple_of(at * 8, 8), 8), :] = piece[0:8, :]
        starts = jnp.where(group == at, piece[8:9, :], starts)
    block[TOK : TOK + 32, :] = rows[...].astype(BF16)
    block[TOK + 32 : TOK + 48, :] = starts.astype(BF16)


def own_body(start_ref, owner, place, t, acc, who):
    who[0:1, :] = owner[...]
    who[1:2, :] = place[...]
    start = start_ref[0]
    spot = lax.broadcasted_iota(I32, (1, TOK), 1)
    lo = jnp.where(spot >= start, start, 0)
    q, g, k, v = (t[:, n * PAIR : (n + 1) * PAIR] for n in range(4))
    slopes, k_part, v_part = attend(q, g, k, v, lo, spot)
    k0, k1 = by_head(k)
    acc[:, 0:PAIR] = dot_tn(slopes[0], k0) + dot_tn(slopes[1], k1)
    acc[:, PAIR : 2 * PAIR] = k_part
    acc[:, 2 * PAIR : 3 * PAIR] = v_part


def state_body(start_ref, m, t, acc_in, acc, pt, qt, rows, res):
    start = start_ref[0]
    chunk = 416
    for h, g in enumerate(by_head(t[:, PAIR : 2 * PAIR])):
        for c in range(0, FEAT, chunk):
            r = dot_nt(m[c : c + chunk, :], g)
            pt[2 * h, c : c + chunk, :] = r[:, 0:PAIR]
            pt[2 * h + 1, c : c + chunk, :] = r[:, PAIR : 2 * PAIR]
    q_t = t[:, 0:PAIR].astype(F32).T
    for h in range(2):
        for half in range(2):
            qt[2 * h + half] = q_t[h * HEAD : (h + 1) * HEAD, half * PAIR : (half + 1) * PAIR]
    sub = lax.broadcasted_iota(I32, (8, PAIR), 0)

    def part(i, carry):
        tiles = HEAD // 8
        sums = [jnp.zeros((8, PAIR), F32) for _ in range(tiles)]
        for a in range(HEAD):
            first = a // 8
            at = a * HEAD - a * (a - 1) // 2 - a % 8
            qa = qt[i, a : a + 1, :]
            row = None
            for b in range(first, tiles):
                tile = pt[i, at + 8 * (b - first) : at + 8 * (b - first) + 8, :]
                if b == first:
                    scale = jnp.where(sub > a % 8, 1.0, jnp.where(sub == a % 8, math.sqrt(0.5), 0.0))
                    tile = tile * scale
                sums[b] = sums[b] + tile * qa
                more = tile * qt[i, 8 * b : 8 * b + 8, :]
                row = more if row is None else row + more
            rows[i, a : a + 1, :] = jnp.sum(row, axis=0, keepdims=True)
        for b in range(tiles):
            res[i, 8 * b : 8 * b + 8, :] = math.sqrt(2.0) * (sums[b] + rows[i, 8 * b : 8 * b + 8, :])
        return carry

    lax.fori_loop(0, 4, part, 0)
    for half in range(2):
        both = jnp.concatenate([res[half], res[2 + half]], 0).T
        spot = half * PAIR + lax.broadcasted_iota(I32, (PAIR, PAIR), 0)
        at = slice(half * PAIR, (half + 1) * PAIR)
        acc[at, 0:PAIR] = acc_in[at, 0:PAIR] + jnp.where(spot < start, both, 0.0)
    acc[:, PAIR : 3 * PAIR] = acc_in[:, PAIR : 3 * PAIR]


def later_part(far, start, t, block):
    x = lax.rem(lax.div(lax.axis_index("seq") + far, ROW), COLS)
    group = lax.shift_right_logical(lax.broadcasted_iota(I32, (16, 2 * PAIR), 0), 2)
    begin = block[TOK + 32 : TOK + 48, :].astype(F32)
    until = jnp.max(jnp.where(group == x, begin, 0.0), axis=0, keepdims=True).astype(I32)
    spot = lax.broadcasted_iota(I32, (1, TOK), 1)
    lo = jnp.where(start == TOK, 0, start)
    hi = jnp.where(spot < until, TOK - 1, -1)
    k, v = t[:, 2 * PAIR : 3 * PAIR], t[:, 3 * PAIR : 4 * PAIR]
    q, g = block[0:TOK, 0:PAIR], block[0:TOK, PAIR : 2 * PAIR]
    _, k_part, v_part = attend(q, g, k, v, lo, hi)
    return k_part, v_part


def later_body(fars, start_ref, t, *rest):
    blocks, out = rest[:-1], rest[-1]
    for n, (far, block) in enumerate(zip(fars, blocks)):
        k_part, v_part = later_part(far, start_ref[0], t, block)
        out[n, :, 0:PAIR] = k_part
        out[n, :, PAIR : 2 * PAIR] = v_part


def add_later(far, count, start, t, block, acc):
    @pl.when(far <= count)
    def _():
        k_part, v_part = later_part(far, start, t, block)
        acc[:, PAIR : 2 * PAIR] += k_part
        acc[:, 2 * PAIR : 3 * PAIR] += v_part


def final_body(done, rest_fars, start_ref, who, t, acc_in, *refs):
    refs = list(refs)
    columns = [refs.pop(0) for _ in range(ROW)]
    parts = [refs.pop(0) for _ in done]
    blocks = [refs.pop(0) for _ in rest_fars]
    acc, longest, count, rows, starts = refs
    shard = lax.axis_index("seq")
    start = start_ref[0]
    z = lax.rem(shard, ROW)
    for block, dz in zip(columns, range(ROW)):
        piece = block[TOK : TOK + 48, :].astype(F32)
        zz = lax.rem(z + dz, ROW)
        for x in range(COLS):
            at = x * ROW + zz
            rows[pl.ds(pl.multiple_of(at * 8, 8), 8), :] = piece[8 * x : 8 * x + 8, :]
            starts[pl.ds(at, 1), :] = piece[32 + 4 * x : 33 + 4 * x, :]
    begin = starts[...]
    sub = lax.broadcasted_iota(I32, (SHARDS, TOK), 0)
    lane = lax.broadcasted_iota(I32, (SHARDS, TOK), 1)
    along = jnp.sum(jnp.where(sub == lane, begin, 0.0), axis=0, keepdims=True)
    stops = (lane > sub) & (lane < SHARDS) & (along < TOK)
    last = jnp.min(jnp.where(stops, lane, SHARDS - 1).astype(F32), axis=1, keepdims=True)
    sub1 = lax.broadcasted_iota(I32, (SHARDS, 1), 0)
    longest[0] = jnp.max(last - sub1.astype(F32)).astype(I32)
    mine = jnp.sum(jnp.where(sub1 == shard, last, 0.0)).astype(I32)
    reach = mine - shard
    count[0] = reach
    owner = who[0:1, :]
    place = who[1:2, :]
    theirs = jnp.sum(jnp.where(sub == owner, begin, 0.0), axis=0, keepdims=True).astype(I32)
    here = owner == shard
    after = (owner > shard) & (owner <= mine) & (place < theirs)
    carry_lo = jnp.where(start == TOK, 0, start)
    lo = jnp.where(here, jnp.where(place >= start, start, 0), carry_lo)
    hi = jnp.where(here, place, jnp.where(after, TOK - 1, -1))
    both = rows[...].astype(BF16)
    k, v = t[:, 2 * PAIR : 3 * PAIR], t[:, 3 * PAIR : 4 * PAIR]
    _, k_part, v_part = attend(both[:, 0:PAIR], both[:, PAIR:], k, v, lo, hi)
    acc[:, 0:PAIR] = acc_in[:, 0:PAIR]
    acc[:, PAIR : 2 * PAIR] = acc_in[:, PAIR : 2 * PAIR] + k_part
    acc[:, 2 * PAIR : 3 * PAIR] = acc_in[:, 2 * PAIR : 3 * PAIR] + v_part
    for fars, part in zip(done, parts):
        for n, far in enumerate(fars):

            @pl.when(far <= reach)
            def _():
                acc[:, PAIR : 3 * PAIR] += part[n]

    for far, block in zip(rest_fars, blocks):
        add_later(far, reach, start, t, block, acc)


def further_body(start_ref, count, base, t, acc_in, *rest):
    blocks, acc = rest[:-1], rest[-1]
    acc[...] = acc_in[...]
    for n, block in enumerate(blocks):
        add_later(base[0] + n + 1, count[0], start_ref[0], t, block, acc)


ACC = jax.ShapeDtypeStruct((TOK, 3 * PAIR), F32)
BLOCK = jax.ShapeDtypeStruct((TOK + 48, 2 * PAIR), BF16)
BLOCK_FLOPS = 8 * 2 * TOK * TOK * PAIR


def later_call(fars, start, t, blocks):
    return call(
        functools.partial(later_body, fars),
        jax.ShapeDtypeStruct((len(fars), TOK, 2 * PAIR), F32),
        [SMEM] + [VMEM] * (1 + len(fars)), VMEM, BLOCK_FLOPS * len(fars), name="later",
    )(start, t, *blocks)


def further_call(start, count, base, t, acc, blocks):
    return call(
        further_body, ACC, [SMEM, SMEM, SMEM] + [VMEM] * (2 + len(blocks)), VMEM,
        BLOCK_FLOPS * len(blocks), aliases={4: 0}, name="further",
    )(start, count, base, t, acc, *blocks)


def shift(x, d):
    return lax.ppermute(x, "seq", [((i + d) % SHARDS, i) for i in range(SHARDS)])


def body(
    queries, keys, values, out_grad, prefix_state, variant_queries, variant_grads,
    variant_owner, variant_position, start,
):
    heads = queries.shape[1] // PAIR
    rows = queries.shape[0]
    anywhere = pl.BlockSpec(memory_space=pltpu.HBM)
    sent, msg = call(
        pack_body,
        (
            jax.ShapeDtypeStruct((heads, rows, 4 * PAIR), BF16),
            jax.ShapeDtypeStruct((16, 2 * PAIR), BF16),
        ),
        [SMEM] + [anywhere] * 4 + [VMEM] * 2, (VMEM, VMEM), 1 << 20,
        scratch=(pltpu.VMEM((4, rows, heads * PAIR), BF16), pltpu.SemaphoreType.DMA((4,))),
        name="pack", vmem=60,
    )(start, queries, out_grad, keys, values, variant_queries, variant_grads)
    msgs = [msg] + [shift(msg, ROW * d) for d in range(1, COLS)]
    t = lax.all_to_all(sent, "heads", split_axis=0, concat_axis=0).reshape(TOK, 4 * PAIR)
    own = call(
        assemble_body, BLOCK, [VMEM] * (1 + COLS), VMEM, 1 << 20,
        scratch=(pltpu.VMEM((32, 2 * PAIR), F32),), name="assemble",
    )(t, *msgs)

    blocks = {far: shift(own, far) for far in (7, 2, 8, 1)}
    for far, via in ((5, 7), (6, 7), (4, 2), (3, 2)):
        blocks[far] = shift(blocks[via], far - via)
    acc, who = call(
        own_body, (ACC, jax.ShapeDtypeStruct((8, TOK), I32)), [SMEM, VMEM, VMEM, VMEM],
        (VMEM, VMEM), BLOCK_FLOPS * 3 // 2, name="own",
    )(start, variant_owner.reshape(1, TOK), variant_position.reshape(1, TOK), t)
    acc = call(
        state_body, ACC, [SMEM, VMEM, VMEM, VMEM], VMEM, 3 * BLOCK_FLOPS,
        scratch=(
            pltpu.VMEM((4, FEAT, PAIR), F32),
            pltpu.VMEM((4, HEAD, PAIR), F32),
            pltpu.VMEM((4, HEAD, PAIR), F32),
            pltpu.VMEM((4, HEAD, PAIR), F32),
        ),
        aliases={3: 0}, name="state",
    )(start, prefix_state[0], t, acc)
    near, second, acc = lax.optimization_barrier((blocks[1], blocks[2], acc))
    blocks[9], blocks[10] = shift(near, ROW), shift(second, ROW)
    done = ((1, 8), (2, 7), (3, 6))
    parts = [later_call(fars, start, t, [blocks[far] for far in fars]) for fars in done]
    left = (4, 5, 9, 10)
    one = jax.ShapeDtypeStruct((1,), I32)
    columns = [own] + [blocks[far] for far in range(1, ROW)]
    acc, longest, count = call(
        functools.partial(final_body, done, left), (ACC, one, one),
        [SMEM] + [VMEM] * (3 + ROW + len(done) + len(left)), (VMEM, SMEM, SMEM), BLOCK_FLOPS,
        scratch=(pltpu.VMEM((TOK, 2 * PAIR), F32), pltpu.VMEM((SHARDS, 2 * PAIR), F32)),
        aliases={3: 0}, name="final",
    )(
        start, who, t, acc,
        *columns, *parts, *[blocks[far] for far in left],
    )
    longest = longest.reshape(())

    def extend(acc):
        def go(carry):
            return carry[0] < longest

        def more(carry):
            base, near, far, acc = carry
            moved = [shift(block, ROW) for block in near]
            acc = further_call(start, count, base.reshape(1), t, acc, moved)
            return base + len(near), far, moved, acc

        near = [blocks[n] for n in (3, 4, 5, 6)]
        far = [blocks[n] for n in (7, 8, 9, 10)]
        return lax.while_loop(go, more, (jnp.int32(REACH), near, far, acc))[3]

    acc = lax.cond(longest > REACH, extend, lambda a: a, acc)
    back = lax.all_to_all(acc.reshape(heads, rows, 3 * PAIR), "heads", split_axis=0, concat_axis=0)
    out = jax.ShapeDtypeStruct((rows, heads * PAIR), F32)
    return tuple(call(unpack_body, (out, out, out), [VMEM], (VMEM,) * 3, 1 << 20, name="unpack")(back))


def solution(mesh):
    tokens = P(("seq", "heads"), None)
    in_specs = (
        tokens, tokens, tokens, tokens, P("seq", None, "heads"), P("seq", "heads"),
        P("seq", "heads"), P(), P(), P("seq"),
    )
    return jax.shard_map(
        body, mesh=mesh, in_specs=in_specs, out_specs=(tokens,) * 3, check_vma=False
    )
```

```python
import functools
import math

import jax
import jax.numpy as jnp
from jax import lax
from jax.experimental import pallas as pl
from jax.experimental.pallas import tpu as pltpu
from jax.sharding import PartitionSpec as P

HEAD = 64
PAIR = 128
TOK = 256
FEAT = 2080
SHARDS = 32
ROW = 8
COLS = SHARDS // ROW
REACH = 10
F32 = jnp.float32
BF16 = jnp.bfloat16
I32 = jnp.int32

VMEM = pl.BlockSpec(memory_space=pltpu.VMEM)
SMEM = pl.BlockSpec(memory_space=pltpu.SMEM)


def call(body, out_shape, in_specs, out_specs, flops, scratch=(), aliases=None, name=None,
         vmem=24):
    return pl.pallas_call(
        body,
        out_shape=out_shape,
        in_specs=in_specs,
        out_specs=out_specs,
        scratch_shapes=list(scratch),
        input_output_aliases=aliases or {},
        compiler_params=pltpu.CompilerParams(vmem_limit_bytes=vmem * 1024 * 1024),
        cost_estimate=pl.CostEstimate(flops=flops, bytes_accessed=1 << 20, transcendentals=0),
        name=name,
    )


def dot_nt(a, b):
    return lax.dot_general(a, b, (((1,), (1,)), ((), ())), preferred_element_type=F32)


def dot_tn(a, b):
    return lax.dot_general(a, b, (((0,), (0,)), ((), ())), preferred_element_type=F32)


def dot_nn(a, b):
    return lax.dot_general(a, b, (((1,), (0,)), ((), ())), preferred_element_type=F32)


def by_head(x):
    low = lax.broadcasted_iota(I32, x.shape, 1) < HEAD
    zero = jnp.zeros_like(x)
    return jnp.where(low, x, zero), jnp.where(low, zero, x)


def attend(q, g, keys, values, lo, hi):
    place = lax.broadcasted_iota(I32, (TOK, q.shape[0]), 0)
    seen = (place >= lo) & (place <= hi)
    slopes, squares = [], []
    for k, v in zip(by_head(keys), by_head(values)):
        score = jnp.where(seen, dot_nt(k, q), 0.0)
        inner = dot_nt(v, g)
        slopes.append((2.0 * score * inner).astype(BF16))
        squares.append((score * score).astype(BF16))
    slope = jnp.concatenate(slopes, 1)
    square = jnp.concatenate(squares, 1)
    k_part = dot_nn(slope, jnp.concatenate(by_head(q), 0))
    v_part = dot_nn(square, jnp.concatenate(by_head(g), 0))
    return slopes, k_part, v_part


def pack_body(start, q, g, k, v, vq, vg, out, msg, buf, sems):
    copies = [
        pltpu.make_async_copy(ref, buf.at[n], sems.at[n]) for n, ref in enumerate((q, g, k, v))
    ]
    for copy in copies:
        copy.start()
    top = jnp.concatenate([vq[...], vg[...]], 1).astype(F32)
    low = jnp.full((8, 2 * PAIR), start[0].astype(F32))
    msg[...] = jnp.concatenate([top, low], 0).astype(BF16)
    for n, copy in enumerate(copies):
        copy.wait()
        for h in range(out.shape[0]):
            out[h, :, n * PAIR : (n + 1) * PAIR] = buf[n, :, h * PAIR : (h + 1) * PAIR]


def unpack_body(x, qo, ko, vo):
    for h in range(x.shape[0]):
        for n, ref in enumerate((qo, ko, vo)):
            ref[:, h * PAIR : (h + 1) * PAIR] = x[h, :, n * PAIR : (n + 1) * PAIR].astype(F32)


def assemble_body(t, *rest):
    msgs, (block, rows) = rest[:COLS], rest[COLS:]
    x = lax.div(lax.axis_index("seq"), ROW)
    block[0:TOK, :] = t[:, 0 : 2 * PAIR]
    group = lax.shift_right_logical(lax.broadcasted_iota(I32, (16, 2 * PAIR), 0), 2)
    starts = jnp.zeros((16, 2 * PAIR), F32)
    for dx, msg in enumerate(msgs):
        at = lax.rem(x + dx, COLS)
        piece = msg[...].astype(F32)
        rows[pl.ds(pl.multiple_of(at * 8, 8), 8), :] = piece[0:8, :]
        starts = jnp.where(group == at, piece[8:9, :], starts)
    block[TOK : TOK + 32, :] = rows[...].astype(BF16)
    block[TOK + 32 : TOK + 48, :] = starts.astype(BF16)


def own_body(start_ref, owner, place, t, acc, who):
    who[0:1, :] = owner[...]
    who[1:2, :] = place[...]
    start = start_ref[0]
    spot = lax.broadcasted_iota(I32, (1, TOK), 1)
    lo = jnp.where(spot >= start, start, 0)
    q, g, k, v = (t[:, n * PAIR : (n + 1) * PAIR] for n in range(4))
    slopes, k_part, v_part = attend(q, g, k, v, lo, spot)
    k0, k1 = by_head(k)
    acc[:, 0:PAIR] = dot_tn(slopes[0], k0) + dot_tn(slopes[1], k1)
    acc[:, PAIR : 2 * PAIR] = k_part
    acc[:, 2 * PAIR : 3 * PAIR] = v_part


def state_body(start_ref, m, t, acc_in, acc, pt, qt, rows, res):
    start = start_ref[0]
    chunk = 416
    for h, g in enumerate(by_head(t[:, PAIR : 2 * PAIR])):
        for c in range(0, FEAT, chunk):
            r = dot_nt(m[c : c + chunk, :], g)
            pt[2 * h, c : c + chunk, :] = r[:, 0:PAIR]
            pt[2 * h + 1, c : c + chunk, :] = r[:, PAIR : 2 * PAIR]
    q_t = t[:, 0:PAIR].astype(F32).T
    for h in range(2):
        for half in range(2):
            qt[2 * h + half] = q_t[h * HEAD : (h + 1) * HEAD, half * PAIR : (half + 1) * PAIR]
    sub = lax.broadcasted_iota(I32, (8, PAIR), 0)

    def part(i, carry):
        tiles = HEAD // 8
        sums = [jnp.zeros((8, PAIR), F32) for _ in range(tiles)]
        for a in range(HEAD):
            first = a // 8
            at = a * HEAD - a * (a - 1) // 2 - a % 8
            qa = qt[i, a : a + 1, :]
            row = None
            for b in range(first, tiles):
                tile = pt[i, at + 8 * (b - first) : at + 8 * (b - first) + 8, :]
                if b == first:
                    scale = jnp.where(sub > a % 8, 1.0, jnp.where(sub == a % 8, math.sqrt(0.5), 0.0))
                    tile = tile * scale
                sums[b] = sums[b] + tile * qa
                more = tile * qt[i, 8 * b : 8 * b + 8, :]
                row = more if row is None else row + more
            rows[i, a : a + 1, :] = jnp.sum(row, axis=0, keepdims=True)
        for b in range(tiles):
            res[i, 8 * b : 8 * b + 8, :] = math.sqrt(2.0) * (sums[b] + rows[i, 8 * b : 8 * b + 8, :])
        return carry

    lax.fori_loop(0, 4, part, 0)
    for half in range(2):
        both = jnp.concatenate([res[half], res[2 + half]], 0).T
        spot = half * PAIR + lax.broadcasted_iota(I32, (PAIR, PAIR), 0)
        at = slice(half * PAIR, (half + 1) * PAIR)
        acc[at, 0:PAIR] = acc_in[at, 0:PAIR] + jnp.where(spot < start, both, 0.0)
    acc[:, PAIR : 3 * PAIR] = acc_in[:, PAIR : 3 * PAIR]


def later_part(far, start, t, block):
    x = lax.rem(lax.div(lax.axis_index("seq") + far, ROW), COLS)
    group = lax.shift_right_logical(lax.broadcasted_iota(I32, (16, 2 * PAIR), 0), 2)
    begin = block[TOK + 32 : TOK + 48, :].astype(F32)
    until = jnp.max(jnp.where(group == x, begin, 0.0), axis=0, keepdims=True).astype(I32)
    spot = lax.broadcasted_iota(I32, (1, TOK), 1)
    lo = jnp.where(start == TOK, 0, start)
    hi = jnp.where(spot < until, TOK - 1, -1)
    k, v = t[:, 2 * PAIR : 3 * PAIR], t[:, 3 * PAIR : 4 * PAIR]
    q, g = block[0:TOK, 0:PAIR], block[0:TOK, PAIR : 2 * PAIR]
    _, k_part, v_part = attend(q, g, k, v, lo, hi)
    return k_part, v_part


def later_body(fars, start_ref, t, *rest):
    blocks, out = rest[:-1], rest[-1]
    for n, (far, block) in enumerate(zip(fars, blocks)):
        k_part, v_part = later_part(far, start_ref[0], t, block)
        out[n, :, 0:PAIR] = k_part
        out[n, :, PAIR : 2 * PAIR] = v_part


def add_later(far, count, start, t, block, acc):
    @pl.when(far <= count)
    def _():
        k_part, v_part = later_part(far, start, t, block)
        acc[:, PAIR : 2 * PAIR] += k_part
        acc[:, 2 * PAIR : 3 * PAIR] += v_part


def final_body(done, rest_fars, start_ref, who, t, acc_in, *refs):
    refs = list(refs)
    columns = [refs.pop(0) for _ in range(ROW)]
    parts = [refs.pop(0) for _ in done]
    blocks = [refs.pop(0) for _ in rest_fars]
    acc, small, longest, count, rows, starts = refs
    shard = lax.axis_index("seq")
    start = start_ref[0]
    z = lax.rem(shard, ROW)
    for block, dz in zip(columns, range(ROW)):
        piece = block[TOK : TOK + 48, :].astype(F32)
        zz = lax.rem(z + dz, ROW)
        for x in range(COLS):
            at = x * ROW + zz
            rows[pl.ds(pl.multiple_of(at * 8, 8), 8), :] = piece[8 * x : 8 * x + 8, :]
            starts[pl.ds(at, 1), :] = piece[32 + 4 * x : 33 + 4 * x, :]
    begin = starts[...]
    sub = lax.broadcasted_iota(I32, (SHARDS, TOK), 0)
    lane = lax.broadcasted_iota(I32, (SHARDS, TOK), 1)
    along = jnp.sum(jnp.where(sub == lane, begin, 0.0), axis=0, keepdims=True)
    stops = (lane > sub) & (lane < SHARDS) & (along < TOK)
    last = jnp.min(jnp.where(stops, lane, SHARDS - 1).astype(F32), axis=1, keepdims=True)
    sub1 = lax.broadcasted_iota(I32, (SHARDS, 1), 0)
    longest[0] = jnp.max(last - sub1.astype(F32)).astype(I32)
    mine = jnp.sum(jnp.where(sub1 == shard, last, 0.0)).astype(I32)
    reach = mine - shard
    count[0] = reach
    owner = who[0:1, :]
    place = who[1:2, :]
    theirs = jnp.sum(jnp.where(sub == owner, begin, 0.0), axis=0, keepdims=True).astype(I32)
    here = owner == shard
    after = (owner > shard) & (owner <= mine) & (place < theirs)
    carry_lo = jnp.where(start == TOK, 0, start)
    lo = jnp.where(here, jnp.where(place >= start, start, 0), carry_lo)
    hi = jnp.where(here, place, jnp.where(after, TOK - 1, -1))
    both = rows[...].astype(BF16)
    k, v = t[:, 2 * PAIR : 3 * PAIR], t[:, 3 * PAIR : 4 * PAIR]
    _, k_part, v_part = attend(both[:, 0:PAIR], both[:, PAIR:], k, v, lo, hi)
    acc[:, 0:PAIR] = acc_in[:, 0:PAIR]
    acc[:, PAIR : 2 * PAIR] = acc_in[:, PAIR : 2 * PAIR] + k_part
    acc[:, 2 * PAIR : 3 * PAIR] = acc_in[:, 2 * PAIR : 3 * PAIR] + v_part
    for fars, part in zip(done, parts):
        for n, far in enumerate(fars):

            @pl.when(far <= reach)
            def _():
                acc[:, PAIR : 3 * PAIR] += part[n]

    for far, block in zip(rest_fars, blocks):
        add_later(far, reach, start, t, block, acc)
    small[...] = acc[...].astype(BF16)


def further_body(start_ref, count, base, t, acc_in, *rest):
    blocks, acc = rest[:-1], rest[-1]
    acc[...] = acc_in[...]
    for n, block in enumerate(blocks):
        add_later(base[0] + n + 1, count[0], start_ref[0], t, block, acc)


ACC = jax.ShapeDtypeStruct((TOK, 3 * PAIR), F32)
BLOCK = jax.ShapeDtypeStruct((TOK + 48, 2 * PAIR), BF16)
BLOCK_FLOPS = 8 * 2 * TOK * TOK * PAIR


def later_call(fars, start, t, blocks):
    return call(
        functools.partial(later_body, fars),
        jax.ShapeDtypeStruct((len(fars), TOK, 2 * PAIR), F32),
        [SMEM] + [VMEM] * (1 + len(fars)), VMEM, BLOCK_FLOPS * len(fars), name="later",
    )(start, t, *blocks)


def further_call(start, count, base, t, acc, blocks):
    return call(
        further_body, ACC, [SMEM, SMEM, SMEM] + [VMEM] * (2 + len(blocks)), VMEM,
        BLOCK_FLOPS * len(blocks), aliases={4: 0}, name="further",
    )(start, count, base, t, acc, *blocks)


def shift(x, d):
    return lax.ppermute(x, "seq", [((i + d) % SHARDS, i) for i in range(SHARDS)])


def body(
    queries, keys, values, out_grad, prefix_state, variant_queries, variant_grads,
    variant_owner, variant_position, start,
):
    heads = queries.shape[1] // PAIR
    rows = queries.shape[0]
    anywhere = pl.BlockSpec(memory_space=pltpu.HBM)
    sent, msg = call(
        pack_body,
        (
            jax.ShapeDtypeStruct((heads, rows, 4 * PAIR), BF16),
            jax.ShapeDtypeStruct((16, 2 * PAIR), BF16),
        ),
        [SMEM] + [anywhere] * 4 + [VMEM] * 2, (VMEM, VMEM), 1 << 20,
        scratch=(pltpu.VMEM((4, rows, heads * PAIR), BF16), pltpu.SemaphoreType.DMA((4,))),
        name="pack", vmem=60,
    )(start, queries, out_grad, keys, values, variant_queries, variant_grads)
    msgs = [msg] + [shift(msg, ROW * d) for d in range(1, COLS)]
    t = lax.all_to_all(sent, "heads", split_axis=0, concat_axis=0).reshape(TOK, 4 * PAIR)
    own = call(
        assemble_body, BLOCK, [VMEM] * (1 + COLS), VMEM, 1 << 20,
        scratch=(pltpu.VMEM((32, 2 * PAIR), F32),), name="assemble",
    )(t, *msgs)

    blocks = {far: shift(own, far) for far in (7, 2, 8, 1)}
    for far, via in ((5, 7), (6, 7), (4, 2), (3, 2)):
        blocks[far] = shift(blocks[via], far - via)
    acc, who = call(
        own_body, (ACC, jax.ShapeDtypeStruct((8, TOK), I32)), [SMEM, VMEM, VMEM, VMEM],
        (VMEM, VMEM), BLOCK_FLOPS * 3 // 2, name="own",
    )(start, variant_owner.reshape(1, TOK), variant_position.reshape(1, TOK), t)
    acc = call(
        state_body, ACC, [SMEM, VMEM, VMEM, VMEM], VMEM, 3 * BLOCK_FLOPS,
        scratch=(
            pltpu.VMEM((4, FEAT, PAIR), F32),
            pltpu.VMEM((4, HEAD, PAIR), F32),
            pltpu.VMEM((4, HEAD, PAIR), F32),
            pltpu.VMEM((4, HEAD, PAIR), F32),
        ),
        aliases={3: 0}, name="state",
    )(start, prefix_state[0], t, acc)
    near, second, acc = lax.optimization_barrier((blocks[1], blocks[2], acc))
    blocks[9], blocks[10] = shift(near, ROW), shift(second, ROW)
    done = ((1, 8), (2, 7), (4, 5))
    parts = [later_call(fars, start, t, [blocks[far] for far in fars]) for fars in done]
    left = (3, 6, 9, 10)
    one = jax.ShapeDtypeStruct((1,), I32)
    columns = [own] + [blocks[far] for far in range(1, ROW)]
    acc, small, longest, count = call(
        functools.partial(final_body, done, left),
        (ACC, jax.ShapeDtypeStruct(ACC.shape, BF16), one, one),
        [SMEM] + [VMEM] * (3 + ROW + len(done) + len(left)), (VMEM, VMEM, SMEM, SMEM),
        BLOCK_FLOPS,
        scratch=(pltpu.VMEM((TOK, 2 * PAIR), F32), pltpu.VMEM((SHARDS, 2 * PAIR), F32)),
        aliases={3: 0}, name="final",
    )(
        start, who, t, acc,
        *columns, *parts, *[blocks[far] for far in left],
    )
    longest = longest.reshape(())

    def extend(acc, small):
        def go(carry):
            return carry[0] < longest

        def more(carry):
            base, near, far, acc = carry
            moved = [shift(block, ROW) for block in near]
            acc = further_call(start, count, base.reshape(1), t, acc, moved)
            return base + len(near), far, moved, acc

        near = [blocks[n] for n in (3, 4, 5, 6)]
        far = [blocks[n] for n in (7, 8, 9, 10)]
        return lax.while_loop(go, more, (jnp.int32(REACH), near, far, acc))[3].astype(BF16)

    small = lax.cond(longest > REACH, extend, lambda acc, small: small, acc, small)
    back = lax.all_to_all(small.reshape(heads, rows, 3 * PAIR), "heads", split_axis=0, concat_axis=0)
    out = jax.ShapeDtypeStruct((rows, heads * PAIR), F32)
    return tuple(call(unpack_body, (out, out, out), [VMEM], (VMEM,) * 3, 1 << 20, name="unpack")(back))


def solution(mesh):
    tokens = P(("seq", "heads"), None)
    in_specs = (
        tokens, tokens, tokens, tokens, P("seq", None, "heads"), P("seq", "heads"),
        P("seq", "heads"), P(), P(), P("seq"),
    )
    return jax.shard_map(
        body, mesh=mesh, in_specs=in_specs, out_specs=(tokens,) * 3, check_vma=False
    )
```

```python
import functools
import math

import jax
import jax.numpy as jnp
from jax import lax
from jax.experimental import pallas as pl
from jax.experimental.pallas import tpu as pltpu
from jax.sharding import PartitionSpec as P

HEAD = 64
PAIR = 128
TOK = 256
FEAT = 2080
SHARDS = 32
ROW = 8
COLS = SHARDS // ROW
REACH = 10
F32 = jnp.float32
BF16 = jnp.bfloat16
I32 = jnp.int32

VMEM = pl.BlockSpec(memory_space=pltpu.VMEM)
SMEM = pl.BlockSpec(memory_space=pltpu.SMEM)


def call(body, out_shape, in_specs, out_specs, flops, scratch=(), aliases=None, name=None,
         vmem=24):
    return pl.pallas_call(
        body,
        out_shape=out_shape,
        in_specs=in_specs,
        out_specs=out_specs,
        scratch_shapes=list(scratch),
        input_output_aliases=aliases or {},
        compiler_params=pltpu.CompilerParams(vmem_limit_bytes=vmem * 1024 * 1024),
        cost_estimate=pl.CostEstimate(flops=flops, bytes_accessed=1 << 20, transcendentals=0),
        name=name,
    )


def dot_nt(a, b):
    return lax.dot_general(a, b, (((1,), (1,)), ((), ())), preferred_element_type=F32)


def dot_tn(a, b):
    return lax.dot_general(a, b, (((0,), (0,)), ((), ())), preferred_element_type=F32)


def dot_nn(a, b):
    return lax.dot_general(a, b, (((1,), (0,)), ((), ())), preferred_element_type=F32)


def by_head(x):
    low = lax.broadcasted_iota(I32, x.shape, 1) < HEAD
    zero = jnp.zeros_like(x)
    return jnp.where(low, x, zero), jnp.where(low, zero, x)


def attend(q, g, keys, values, lo, hi):
    place = lax.broadcasted_iota(I32, (TOK, q.shape[0]), 0)
    seen = (place >= lo) & (place <= hi)
    slopes, squares = [], []
    for k, v in zip(by_head(keys), by_head(values)):
        score = jnp.where(seen, dot_nt(k, q), 0.0)
        inner = dot_nt(v, g)
        slopes.append((2.0 * score * inner).astype(BF16))
        squares.append((score * score).astype(BF16))
    slope = jnp.concatenate(slopes, 1)
    square = jnp.concatenate(squares, 1)
    k_part = dot_nn(slope, jnp.concatenate(by_head(q), 0))
    v_part = dot_nn(square, jnp.concatenate(by_head(g), 0))
    return slopes, k_part, v_part


def pack_body(start, q, g, k, v, vq, vg, out, msg, buf, sems):
    copies = [
        pltpu.make_async_copy(ref, buf.at[n], sems.at[n]) for n, ref in enumerate((q, g, k, v))
    ]
    for copy in copies:
        copy.start()
    top = jnp.concatenate([vq[...], vg[...]], 1).astype(F32)
    low = jnp.full((8, 2 * PAIR), start[0].astype(F32))
    msg[...] = jnp.concatenate([top, low], 0).astype(BF16)
    for n, copy in enumerate(copies):
        copy.wait()
        for h in range(out.shape[0]):
            out[h, :, n * PAIR : (n + 1) * PAIR] = buf[n, :, h * PAIR : (h + 1) * PAIR]


def unpack_body(x, qo, ko, vo):
    for h in range(x.shape[0]):
        for n, ref in enumerate((qo, ko, vo)):
            ref[:, h * PAIR : (h + 1) * PAIR] = x[h, :, n * PAIR : (n + 1) * PAIR].astype(F32)


def assemble_body(t, *rest):
    msgs, (block, rows) = rest[:2], rest[2:]
    x = lax.div(lax.axis_index("seq"), ROW)
    block[0:TOK, :] = t[:, 0 : 2 * PAIR]
    group = lax.shift_right_logical(lax.broadcasted_iota(I32, (16, 2 * PAIR), 0), 2)
    starts = jnp.zeros((16, 2 * PAIR), F32)
    for dx in range(COLS):
        at = lax.rem(x + dx, COLS)
        piece = msgs[dx % 2][dx // 2 * 16 : dx // 2 * 16 + 16, :].astype(F32)
        rows[pl.ds(pl.multiple_of(at * 8, 8), 8), :] = piece[0:8, :]
        starts = jnp.where(group == at, piece[8:9, :], starts)
    block[TOK : TOK + 32, :] = rows[...].astype(BF16)
    block[TOK + 32 : TOK + 48, :] = starts.astype(BF16)


def own_body(start_ref, owner, place, t, acc, who):
    who[0:1, :] = owner[...]
    who[1:2, :] = place[...]
    start = start_ref[0]
    spot = lax.broadcasted_iota(I32, (1, TOK), 1)
    lo = jnp.where(spot >= start, start, 0)
    q, g, k, v = (t[:, n * PAIR : (n + 1) * PAIR] for n in range(4))
    slopes, k_part, v_part = attend(q, g, k, v, lo, spot)
    k0, k1 = by_head(k)
    acc[:, 0:PAIR] = dot_tn(slopes[0], k0) + dot_tn(slopes[1], k1)
    acc[:, PAIR : 2 * PAIR] = k_part
    acc[:, 2 * PAIR : 3 * PAIR] = v_part


def state_body(start_ref, m, t, acc_in, acc, pt, qt, rows, res):
    start = start_ref[0]
    chunk = 416
    for h, g in enumerate(by_head(t[:, PAIR : 2 * PAIR])):
        for c in range(0, FEAT, chunk):
            r = dot_nt(m[c : c + chunk, :], g)
            pt[2 * h, c : c + chunk, :] = r[:, 0:PAIR]
            pt[2 * h + 1, c : c + chunk, :] = r[:, PAIR : 2 * PAIR]
    q_t = t[:, 0:PAIR].astype(F32).T
    for h in range(2):
        for half in range(2):
            qt[2 * h + half] = q_t[h * HEAD : (h + 1) * HEAD, half * PAIR : (half + 1) * PAIR]
    sub = lax.broadcasted_iota(I32, (8, PAIR), 0)

    def part(i, carry):
        tiles = HEAD // 8
        sums = [jnp.zeros((8, PAIR), F32) for _ in range(tiles)]
        for a in range(HEAD):
            first = a // 8
            at = a * HEAD - a * (a - 1) // 2 - a % 8
            qa = qt[i, a : a + 1, :]
            row = None
            for b in range(first, tiles):
                tile = pt[i, at + 8 * (b - first) : at + 8 * (b - first) + 8, :]
                if b == first:
                    scale = jnp.where(sub > a % 8, 1.0, jnp.where(sub == a % 8, math.sqrt(0.5), 0.0))
                    tile = tile * scale
                sums[b] = sums[b] + tile * qa
                more = tile * qt[i, 8 * b : 8 * b + 8, :]
                row = more if row is None else row + more
            rows[i, a : a + 1, :] = jnp.sum(row, axis=0, keepdims=True)
        for b in range(tiles):
            res[i, 8 * b : 8 * b + 8, :] = math.sqrt(2.0) * (sums[b] + rows[i, 8 * b : 8 * b + 8, :])
        return carry

    lax.fori_loop(0, 4, part, 0)
    for half in range(2):
        both = jnp.concatenate([res[half], res[2 + half]], 0).T
        spot = half * PAIR + lax.broadcasted_iota(I32, (PAIR, PAIR), 0)
        at = slice(half * PAIR, (half + 1) * PAIR)
        acc[at, 0:PAIR] = acc_in[at, 0:PAIR] + jnp.where(spot < start, both, 0.0)
    acc[:, PAIR : 3 * PAIR] = acc_in[:, PAIR : 3 * PAIR]


def later_part(far, start, t, block):
    x = lax.rem(lax.div(lax.axis_index("seq") + far, ROW), COLS)
    group = lax.shift_right_logical(lax.broadcasted_iota(I32, (16, 2 * PAIR), 0), 2)
    begin = block[TOK + 32 : TOK + 48, :].astype(F32)
    until = jnp.max(jnp.where(group == x, begin, 0.0), axis=0, keepdims=True).astype(I32)
    spot = lax.broadcasted_iota(I32, (1, TOK), 1)
    lo = jnp.where(start == TOK, 0, start)
    hi = jnp.where(spot < until, TOK - 1, -1)
    k, v = t[:, 2 * PAIR : 3 * PAIR], t[:, 3 * PAIR : 4 * PAIR]
    q, g = block[0:TOK, 0:PAIR], block[0:TOK, PAIR : 2 * PAIR]
    _, k_part, v_part = attend(q, g, k, v, lo, hi)
    return k_part, v_part


def later_body(fars, start_ref, t, *rest):
    blocks, out = rest[:-1], rest[-1]
    for n, (far, block) in enumerate(zip(fars, blocks)):
        k_part, v_part = later_part(far, start_ref[0], t, block)
        out[n, :, 0:PAIR] = k_part
        out[n, :, PAIR : 2 * PAIR] = v_part


def add_later(far, count, start, t, block, acc):
    @pl.when(far <= count)
    def _():
        k_part, v_part = later_part(far, start, t, block)
        acc[:, PAIR : 2 * PAIR] += k_part
        acc[:, 2 * PAIR : 3 * PAIR] += v_part


def final_body(done, rest_fars, start_ref, who, t, acc_in, *refs):
    refs = list(refs)
    columns = [refs.pop(0) for _ in range(ROW)]
    parts = [refs.pop(0) for _ in done]
    blocks = [refs.pop(0) for _ in rest_fars]
    acc, small, longest, count, rows, starts = refs
    shard = lax.axis_index("seq")
    start = start_ref[0]
    z = lax.rem(shard, ROW)
    for block, dz in zip(columns, range(ROW)):
        piece = block[TOK : TOK + 48, :].astype(F32)
        zz = lax.rem(z + dz, ROW)
        for x in range(COLS):
            at = x * ROW + zz
            rows[pl.ds(pl.multiple_of(at * 8, 8), 8), :] = piece[8 * x : 8 * x + 8, :]
            starts[pl.ds(at, 1), :] = piece[32 + 4 * x : 33 + 4 * x, :]
    begin = starts[...]
    sub = lax.broadcasted_iota(I32, (SHARDS, TOK), 0)
    lane = lax.broadcasted_iota(I32, (SHARDS, TOK), 1)
    along = jnp.sum(jnp.where(sub == lane, begin, 0.0), axis=0, keepdims=True)
    stops = (lane > sub) & (lane < SHARDS) & (along < TOK)
    last = jnp.min(jnp.where(stops, lane, SHARDS - 1).astype(F32), axis=1, keepdims=True)
    sub1 = lax.broadcasted_iota(I32, (SHARDS, 1), 0)
    longest[0] = jnp.max(last - sub1.astype(F32)).astype(I32)
    mine = jnp.sum(jnp.where(sub1 == shard, last, 0.0)).astype(I32)
    reach = mine - shard
    count[0] = reach
    owner = who[0:1, :]
    place = who[1:2, :]
    theirs = jnp.sum(jnp.where(sub == owner, begin, 0.0), axis=0, keepdims=True).astype(I32)
    here = owner == shard
    after = (owner > shard) & (owner <= mine) & (place < theirs)
    carry_lo = jnp.where(start == TOK, 0, start)
    lo = jnp.where(here, jnp.where(place >= start, start, 0), carry_lo)
    hi = jnp.where(here, place, jnp.where(after, TOK - 1, -1))
    both = rows[...].astype(BF16)
    k, v = t[:, 2 * PAIR : 3 * PAIR], t[:, 3 * PAIR : 4 * PAIR]
    _, k_part, v_part = attend(both[:, 0:PAIR], both[:, PAIR:], k, v, lo, hi)
    acc[:, 0:PAIR] = acc_in[:, 0:PAIR]
    acc[:, PAIR : 2 * PAIR] = acc_in[:, PAIR : 2 * PAIR] + k_part
    acc[:, 2 * PAIR : 3 * PAIR] = acc_in[:, 2 * PAIR : 3 * PAIR] + v_part
    for fars, part in zip(done, parts):
        for n, far in enumerate(fars):

            @pl.when(far <= reach)
            def _():
                acc[:, PAIR : 3 * PAIR] += part[n]

    for far, block in zip(rest_fars, blocks):
        add_later(far, reach, start, t, block, acc)
    small[...] = acc[...].astype(BF16)


def further_body(start_ref, count, base, t, acc_in, *rest):
    blocks, acc = rest[:-1], rest[-1]
    acc[...] = acc_in[...]
    for n, block in enumerate(blocks):
        add_later(base[0] + n + 1, count[0], start_ref[0], t, block, acc)


ACC = jax.ShapeDtypeStruct((TOK, 3 * PAIR), F32)
BLOCK = jax.ShapeDtypeStruct((TOK + 48, 2 * PAIR), BF16)
BLOCK_FLOPS = 8 * 2 * TOK * TOK * PAIR


def later_call(fars, start, t, blocks):
    return call(
        functools.partial(later_body, fars),
        jax.ShapeDtypeStruct((len(fars), TOK, 2 * PAIR), F32),
        [SMEM] + [VMEM] * (1 + len(fars)), VMEM, BLOCK_FLOPS * len(fars), name="later",
    )(start, t, *blocks)


def further_call(start, count, base, t, acc, blocks):
    return call(
        further_body, ACC, [SMEM, SMEM, SMEM] + [VMEM] * (2 + len(blocks)), VMEM,
        BLOCK_FLOPS * len(blocks), aliases={4: 0}, name="further",
    )(start, count, base, t, acc, *blocks)


def shift(x, d):
    return lax.ppermute(x, "seq", [((i + d) % SHARDS, i) for i in range(SHARDS)])


def body(
    queries, keys, values, out_grad, prefix_state, variant_queries, variant_grads,
    variant_owner, variant_position, start,
):
    heads = queries.shape[1] // PAIR
    rows = queries.shape[0]
    anywhere = pl.BlockSpec(memory_space=pltpu.HBM)
    sent, msg = call(
        pack_body,
        (
            jax.ShapeDtypeStruct((heads, rows, 4 * PAIR), BF16),
            jax.ShapeDtypeStruct((16, 2 * PAIR), BF16),
        ),
        [SMEM] + [anywhere] * 4 + [VMEM] * 2, (VMEM, VMEM), 1 << 20,
        scratch=(pltpu.VMEM((4, rows, heads * PAIR), BF16), pltpu.SemaphoreType.DMA((4,))),
        name="pack", vmem=60,
    )(start, queries, out_grad, keys, values, variant_queries, variant_grads)
    msgs = jnp.concatenate([msg, shift(msg, 2 * ROW)], 0)
    msgs = (msgs, shift(msgs, ROW))
    t = lax.all_to_all(sent, "heads", split_axis=0, concat_axis=0).reshape(TOK, 4 * PAIR)
    own = call(
        assemble_body, BLOCK, [VMEM] * 3, VMEM, 1 << 20,
        scratch=(pltpu.VMEM((32, 2 * PAIR), F32),), name="assemble",
    )(t, *msgs)

    blocks = {far: shift(own, far) for far in (8, 2, 1)}
    for far, via in ((6, 8), (7, 8), (4, 2), (3, 2), (5, 6)):
        blocks[far] = shift(blocks[via], far - via)
    acc, who = call(
        own_body, (ACC, jax.ShapeDtypeStruct((8, TOK), I32)), [SMEM, VMEM, VMEM, VMEM],
        (VMEM, VMEM), BLOCK_FLOPS * 3 // 2, name="own",
    )(start, variant_owner.reshape(1, TOK), variant_position.reshape(1, TOK), t)
    acc = call(
        state_body, ACC, [SMEM, VMEM, VMEM, VMEM], VMEM, 3 * BLOCK_FLOPS,
        scratch=(
            pltpu.VMEM((4, FEAT, PAIR), F32),
            pltpu.VMEM((4, HEAD, PAIR), F32),
            pltpu.VMEM((4, HEAD, PAIR), F32),
            pltpu.VMEM((4, HEAD, PAIR), F32),
        ),
        aliases={3: 0}, name="state",
    )(start, prefix_state[0], t, acc)
    near, second, acc, _ = lax.optimization_barrier((blocks[1], blocks[2], acc, blocks[6]))
    blocks[9], blocks[10] = shift(near, ROW), shift(second, ROW)
    done = ((1, 8), (2, 7), (4, 6))
    parts = [later_call(fars, start, t, [blocks[far] for far in fars]) for fars in done]
    left = (3, 5, 9, 10)
    one = jax.ShapeDtypeStruct((1,), I32)
    columns = [own] + [blocks[far] for far in range(1, ROW)]
    acc, small, longest, count = call(
        functools.partial(final_body, done, left),
        (ACC, jax.ShapeDtypeStruct(ACC.shape, BF16), one, one),
        [SMEM] + [VMEM] * (3 + ROW + len(done) + len(left)), (VMEM, VMEM, SMEM, SMEM),
        BLOCK_FLOPS,
        scratch=(pltpu.VMEM((TOK, 2 * PAIR), F32), pltpu.VMEM((SHARDS, 2 * PAIR), F32)),
        aliases={3: 0}, name="final",
    )(
        start, who, t, acc,
        *columns, *parts, *[blocks[far] for far in left],
    )
    longest = longest.reshape(())

    def extend(acc, small):
        def go(carry):
            return carry[0] < longest

        def more(carry):
            base, near, far, acc = carry
            moved = [shift(block, ROW) for block in near]
            acc = further_call(start, count, base.reshape(1), t, acc, moved)
            return base + len(near), far, moved, acc

        near = [blocks[n] for n in (3, 4, 5, 6)]
        far = [blocks[n] for n in (7, 8, 9, 10)]
        return lax.while_loop(go, more, (jnp.int32(REACH), near, far, acc))[3].astype(BF16)

    small = lax.cond(longest > REACH, extend, lambda acc, small: small, acc, small)
    back = lax.all_to_all(small.reshape(heads, rows, 3 * PAIR), "heads", split_axis=0, concat_axis=0)
    out = jax.ShapeDtypeStruct((rows, heads * PAIR), F32)
    return tuple(call(unpack_body, (out, out, out), [VMEM], (VMEM,) * 3, 1 << 20, name="unpack")(back))


def solution(mesh):
    tokens = P(("seq", "heads"), None)
    in_specs = (
        tokens, tokens, tokens, tokens, P("seq", None, "heads"), P("seq", "heads"),
        P("seq", "heads"), P(), P(), P("seq"),
    )
    return jax.shard_map(
        body, mesh=mesh, in_specs=in_specs, out_specs=(tokens,) * 3, check_vma=False
    )
```

```python
import functools
import math

import jax
import jax.numpy as jnp
from jax import lax
from jax.experimental import pallas as pl
from jax.experimental.pallas import tpu as pltpu
from jax.sharding import PartitionSpec as P

HEAD = 64
PAIR = 128
TOK = 256
FEAT = 2080
SHARDS = 32
ROW = 8
COLS = SHARDS // ROW
REACH = 10
F32 = jnp.float32
BF16 = jnp.bfloat16
I32 = jnp.int32

VMEM = pl.BlockSpec(memory_space=pltpu.VMEM)
SMEM = pl.BlockSpec(memory_space=pltpu.SMEM)


def call(body, out_shape, in_specs, out_specs, flops, scratch=(), aliases=None, name=None,
         vmem=24):
    return pl.pallas_call(
        body,
        out_shape=out_shape,
        in_specs=in_specs,
        out_specs=out_specs,
        scratch_shapes=list(scratch),
        input_output_aliases=aliases or {},
        compiler_params=pltpu.CompilerParams(vmem_limit_bytes=vmem * 1024 * 1024),
        cost_estimate=pl.CostEstimate(flops=flops, bytes_accessed=1 << 20, transcendentals=0),
        name=name,
    )


def dot_nt(a, b):
    return lax.dot_general(a, b, (((1,), (1,)), ((), ())), preferred_element_type=F32)


def dot_tn(a, b):
    return lax.dot_general(a, b, (((0,), (0,)), ((), ())), preferred_element_type=F32)


def dot_nn(a, b):
    return lax.dot_general(a, b, (((1,), (0,)), ((), ())), preferred_element_type=F32)


def by_head(x):
    low = lax.broadcasted_iota(I32, x.shape, 1) < HEAD
    zero = jnp.zeros_like(x)
    return jnp.where(low, x, zero), jnp.where(low, zero, x)


def attend(q, g, keys, values, lo, hi):
    place = lax.broadcasted_iota(I32, (TOK, q.shape[0]), 0)
    seen = (place >= lo) & (place <= hi)
    slopes, squares = [], []
    for k, v in zip(by_head(keys), by_head(values)):
        score = jnp.where(seen, dot_nt(k, q), 0.0)
        inner = dot_nt(v, g)
        slopes.append((2.0 * score * inner).astype(BF16))
        squares.append((score * score).astype(BF16))
    slope = jnp.concatenate(slopes, 1)
    square = jnp.concatenate(squares, 1)
    k_part = dot_nn(slope, jnp.concatenate(by_head(q), 0))
    v_part = dot_nn(square, jnp.concatenate(by_head(g), 0))
    return slopes, k_part, v_part


def pack_body(start, q, g, k, v, vq, vg, out, msg, sems):
    copies = [
        pltpu.make_async_copy(
            ref.at[:, h * PAIR : (h + 1) * PAIR],
            out.at[h, :, n * PAIR : (n + 1) * PAIR],
            sems.at[n, h],
        )
        for n, ref in enumerate((q, g, k, v))
        for h in range(out.shape[0])
    ]
    for copy in copies:
        copy.start()
    top = jnp.concatenate([vq[...], vg[...]], 1).astype(F32)
    low = jnp.full((8, 2 * PAIR), start[0].astype(F32))
    msg[...] = jnp.concatenate([top, low], 0).astype(BF16)
    for copy in copies:
        copy.wait()


def unpack_body(x, qo, ko, vo):
    for h in range(x.shape[0]):
        for n, ref in enumerate((qo, ko, vo)):
            ref[:, h * PAIR : (h + 1) * PAIR] = x[h, :, n * PAIR : (n + 1) * PAIR].astype(F32)


def assemble_body(t, *rest):
    msgs, (block, rows) = rest[:COLS], rest[COLS:]
    x = lax.div(lax.axis_index("seq"), ROW)
    block[0:TOK, :] = t[:, 0 : 2 * PAIR]
    group = lax.shift_right_logical(lax.broadcasted_iota(I32, (16, 2 * PAIR), 0), 2)
    starts = jnp.zeros((16, 2 * PAIR), F32)
    for dx, msg in enumerate(msgs):
        at = lax.rem(x + dx, COLS)
        piece = msg[...].astype(F32)
        rows[pl.ds(pl.multiple_of(at * 8, 8), 8), :] = piece[0:8, :]
        starts = jnp.where(group == at, piece[8:9, :], starts)
    block[TOK : TOK + 32, :] = rows[...].astype(BF16)
    block[TOK + 32 : TOK + 48, :] = starts.astype(BF16)


def own_body(start_ref, owner, place, t, acc, who):
    who[0:1, :] = owner[...]
    who[1:2, :] = place[...]
    start = start_ref[0]
    spot = lax.broadcasted_iota(I32, (1, TOK), 1)
    lo = jnp.where(spot >= start, start, 0)
    q, g, k, v = (t[:, n * PAIR : (n + 1) * PAIR] for n in range(4))
    slopes, k_part, v_part = attend(q, g, k, v, lo, spot)
    k0, k1 = by_head(k)
    acc[:, 0:PAIR] = dot_tn(slopes[0], k0) + dot_tn(slopes[1], k1)
    acc[:, PAIR : 2 * PAIR] = k_part
    acc[:, 2 * PAIR : 3 * PAIR] = v_part


def state_body(start_ref, m, t, acc_in, acc, pt, qt, rows, res):
    start = start_ref[0]
    chunk = 416
    for h, g in enumerate(by_head(t[:, PAIR : 2 * PAIR])):
        for c in range(0, FEAT, chunk):
            r = dot_nt(m[c : c + chunk, :], g)
            pt[2 * h, c : c + chunk, :] = r[:, 0:PAIR]
            pt[2 * h + 1, c : c + chunk, :] = r[:, PAIR : 2 * PAIR]
    q_t = t[:, 0:PAIR].astype(F32).T
    for h in range(2):
        for half in range(2):
            qt[2 * h + half] = q_t[h * HEAD : (h + 1) * HEAD, half * PAIR : (half + 1) * PAIR]
    sub = lax.broadcasted_iota(I32, (8, PAIR), 0)

    def part(i, carry):
        tiles = HEAD // 8
        sums = [jnp.zeros((8, PAIR), F32) for _ in range(tiles)]
        for a in range(HEAD):
            first = a // 8
            at = a * HEAD - a * (a - 1) // 2 - a % 8
            qa = qt[i, a : a + 1, :]
            row = None
            for b in range(first, tiles):
                tile = pt[i, at + 8 * (b - first) : at + 8 * (b - first) + 8, :]
                if b == first:
                    scale = jnp.where(sub > a % 8, 1.0, jnp.where(sub == a % 8, math.sqrt(0.5), 0.0))
                    tile = tile * scale
                sums[b] = sums[b] + tile * qa
                more = tile * qt[i, 8 * b : 8 * b + 8, :]
                row = more if row is None else row + more
            rows[i, a : a + 1, :] = jnp.sum(row, axis=0, keepdims=True)
        for b in range(tiles):
            res[i, 8 * b : 8 * b + 8, :] = math.sqrt(2.0) * (sums[b] + rows[i, 8 * b : 8 * b + 8, :])
        return carry

    lax.fori_loop(0, 4, part, 0)
    for half in range(2):
        both = jnp.concatenate([res[half], res[2 + half]], 0).T
        spot = half * PAIR + lax.broadcasted_iota(I32, (PAIR, PAIR), 0)
        at = slice(half * PAIR, (half + 1) * PAIR)
        acc[at, 0:PAIR] = acc_in[at, 0:PAIR] + jnp.where(spot < start, both, 0.0)
    acc[:, PAIR : 3 * PAIR] = acc_in[:, PAIR : 3 * PAIR]


def later_part(far, start, t, block):
    x = lax.rem(lax.div(lax.axis_index("seq") + far, ROW), COLS)
    group = lax.shift_right_logical(lax.broadcasted_iota(I32, (16, 2 * PAIR), 0), 2)
    begin = block[TOK + 32 : TOK + 48, :].astype(F32)
    until = jnp.max(jnp.where(group == x, begin, 0.0), axis=0, keepdims=True).astype(I32)
    spot = lax.broadcasted_iota(I32, (1, TOK), 1)
    lo = jnp.where(start == TOK, 0, start)
    hi = jnp.where(spot < until, TOK - 1, -1)
    k, v = t[:, 2 * PAIR : 3 * PAIR], t[:, 3 * PAIR : 4 * PAIR]
    q, g = block[0:TOK, 0:PAIR], block[0:TOK, PAIR : 2 * PAIR]
    _, k_part, v_part = attend(q, g, k, v, lo, hi)
    return k_part, v_part


def later_body(fars, start_ref, t, *rest):
    blocks, out = rest[:-1], rest[-1]
    for n, (far, block) in enumerate(zip(fars, blocks)):
        k_part, v_part = later_part(far, start_ref[0], t, block)
        out[n, :, 0:PAIR] = k_part
        out[n, :, PAIR : 2 * PAIR] = v_part


def add_later(far, count, start, t, block, acc):
    @pl.when(far <= count)
    def _():
        k_part, v_part = later_part(far, start, t, block)
        acc[:, PAIR : 2 * PAIR] += k_part
        acc[:, 2 * PAIR : 3 * PAIR] += v_part


def final_body(done, rest_fars, start_ref, who, t, acc_in, *refs):
    refs = list(refs)
    columns = [refs.pop(0) for _ in range(ROW)]
    parts = [refs.pop(0) for _ in done]
    blocks = [refs.pop(0) for _ in rest_fars]
    acc, small, longest, count, rows, starts = refs
    shard = lax.axis_index("seq")
    start = start_ref[0]
    z = lax.rem(shard, ROW)
    for block, dz in zip(columns, range(ROW)):
        piece = block[TOK : TOK + 48, :].astype(F32)
        zz = lax.rem(z + dz, ROW)
        for x in range(COLS):
            at = x * ROW + zz
            rows[pl.ds(pl.multiple_of(at * 8, 8), 8), :] = piece[8 * x : 8 * x + 8, :]
            starts[pl.ds(at, 1), :] = piece[32 + 4 * x : 33 + 4 * x, :]
    begin = starts[...]
    sub = lax.broadcasted_iota(I32, (SHARDS, TOK), 0)
    lane = lax.broadcasted_iota(I32, (SHARDS, TOK), 1)
    along = jnp.sum(jnp.where(sub == lane, begin, 0.0), axis=0, keepdims=True)
    stops = (lane > sub) & (lane < SHARDS) & (along < TOK)
    last = jnp.min(jnp.where(stops, lane, SHARDS - 1).astype(F32), axis=1, keepdims=True)
    sub1 = lax.broadcasted_iota(I32, (SHARDS, 1), 0)
    longest[0] = jnp.max(last - sub1.astype(F32)).astype(I32)
    mine = jnp.sum(jnp.where(sub1 == shard, last, 0.0)).astype(I32)
    reach = mine - shard
    count[0] = reach
    owner = who[0:1, :]
    place = who[1:2, :]
    theirs = jnp.sum(jnp.where(sub == owner, begin, 0.0), axis=0, keepdims=True).astype(I32)
    here = owner == shard
    after = (owner > shard) & (owner <= mine) & (place < theirs)
    carry_lo = jnp.where(start == TOK, 0, start)
    lo = jnp.where(here, jnp.where(place >= start, start, 0), carry_lo)
    hi = jnp.where(here, place, jnp.where(after, TOK - 1, -1))
    both = rows[...].astype(BF16)
    k, v = t[:, 2 * PAIR : 3 * PAIR], t[:, 3 * PAIR : 4 * PAIR]
    _, k_part, v_part = attend(both[:, 0:PAIR], both[:, PAIR:], k, v, lo, hi)
    acc[:, 0:PAIR] = acc_in[:, 0:PAIR]
    acc[:, PAIR : 2 * PAIR] = acc_in[:, PAIR : 2 * PAIR] + k_part
    acc[:, 2 * PAIR : 3 * PAIR] = acc_in[:, 2 * PAIR : 3 * PAIR] + v_part
    for fars, part in zip(done, parts):
        for n, far in enumerate(fars):

            @pl.when(far <= reach)
            def _():
                acc[:, PAIR : 3 * PAIR] += part[n]

    for far, block in zip(rest_fars, blocks):
        add_later(far, reach, start, t, block, acc)
    small[...] = acc[...].astype(BF16)


def further_body(start_ref, count, base, t, acc_in, *rest):
    blocks, acc = rest[:-1], rest[-1]
    acc[...] = acc_in[...]
    for n, block in enumerate(blocks):
        add_later(base[0] + n + 1, count[0], start_ref[0], t, block, acc)


ACC = jax.ShapeDtypeStruct((TOK, 3 * PAIR), F32)
BLOCK = jax.ShapeDtypeStruct((TOK + 48, 2 * PAIR), BF16)
BLOCK_FLOPS = 8 * 2 * TOK * TOK * PAIR


def later_call(fars, start, t, blocks):
    return call(
        functools.partial(later_body, fars),
        jax.ShapeDtypeStruct((len(fars), TOK, 2 * PAIR), F32),
        [SMEM] + [VMEM] * (1 + len(fars)), VMEM, BLOCK_FLOPS * len(fars), name="later",
    )(start, t, *blocks)


def further_call(start, count, base, t, acc, blocks):
    return call(
        further_body, ACC, [SMEM, SMEM, SMEM] + [VMEM] * (2 + len(blocks)), VMEM,
        BLOCK_FLOPS * len(blocks), aliases={4: 0}, name="further",
    )(start, count, base, t, acc, *blocks)


def shift(x, d):
    return lax.ppermute(x, "seq", [((i + d) % SHARDS, i) for i in range(SHARDS)])


def body(
    queries, keys, values, out_grad, prefix_state, variant_queries, variant_grads,
    variant_owner, variant_position, start,
):
    heads = queries.shape[1] // PAIR
    rows = queries.shape[0]
    anywhere = pl.BlockSpec(memory_space=pltpu.HBM)
    sent, msg = call(
        pack_body,
        (
            jax.ShapeDtypeStruct((heads, rows, 4 * PAIR), BF16),
            jax.ShapeDtypeStruct((16, 2 * PAIR), BF16),
        ),
        [SMEM] + [anywhere] * 4 + [VMEM] * 2, (anywhere, VMEM), 1 << 20,
        scratch=(pltpu.SemaphoreType.DMA((4, heads)),),
        name="pack", vmem=60,
    )(start, queries, out_grad, keys, values, variant_queries, variant_grads)
    msgs = [msg] + [shift(msg, ROW * d) for d in range(1, COLS)]
    t = lax.all_to_all(sent, "heads", split_axis=0, concat_axis=0).reshape(TOK, 4 * PAIR)
    own = call(
        assemble_body, BLOCK, [VMEM] * (1 + COLS), VMEM, 1 << 20,
        scratch=(pltpu.VMEM((32, 2 * PAIR), F32),), name="assemble",
    )(t, *msgs)

    blocks = {far: shift(own, far) for far in (7, 2, 8, 1)}
    for far, via in ((5, 7), (6, 7), (4, 2), (3, 2)):
        blocks[far] = shift(blocks[via], far - via)
    acc, who = call(
        own_body, (ACC, jax.ShapeDtypeStruct((8, TOK), I32)), [SMEM, VMEM, VMEM, VMEM],
        (VMEM, VMEM), BLOCK_FLOPS * 3 // 2, name="own",
    )(start, variant_owner.reshape(1, TOK), variant_position.reshape(1, TOK), t)
    acc = call(
        state_body, ACC, [SMEM, VMEM, VMEM, VMEM], VMEM, 3 * BLOCK_FLOPS,
        scratch=(
            pltpu.VMEM((4, FEAT, PAIR), F32),
            pltpu.VMEM((4, HEAD, PAIR), F32),
            pltpu.VMEM((4, HEAD, PAIR), F32),
            pltpu.VMEM((4, HEAD, PAIR), F32),
        ),
        aliases={3: 0}, name="state",
    )(start, prefix_state[0], t, acc)
    near, second = lax.optimization_barrier((blocks[1], blocks[2]))
    blocks[9], blocks[10] = shift(near, ROW), shift(second, ROW)
    done = ((1, 8), (2, 7), (4, 5))
    parts = [later_call(fars, start, t, [blocks[far] for far in fars]) for fars in done]
    left = (3, 6, 9, 10)
    one = jax.ShapeDtypeStruct((1,), I32)
    columns = [own] + [blocks[far] for far in range(1, ROW)]
    acc, small, longest, count = call(
        functools.partial(final_body, done, left),
        (ACC, jax.ShapeDtypeStruct(ACC.shape, BF16), one, one),
        [SMEM] + [VMEM] * (3 + ROW + len(done) + len(left)), (VMEM, VMEM, SMEM, SMEM),
        BLOCK_FLOPS,
        scratch=(pltpu.VMEM((TOK, 2 * PAIR), F32), pltpu.VMEM((SHARDS, 2 * PAIR), F32)),
        aliases={3: 0}, name="final",
    )(
        start, who, t, acc,
        *columns, *parts, *[blocks[far] for far in left],
    )
    longest = longest.reshape(())

    def extend(acc, small):
        def go(carry):
            return carry[0] < longest

        def more(carry):
            base, near, far, acc = carry
            moved = [shift(block, ROW) for block in near]
            acc = further_call(start, count, base.reshape(1), t, acc, moved)
            return base + len(near), far, moved, acc

        near = [blocks[n] for n in (3, 4, 5, 6)]
        far = [blocks[n] for n in (7, 8, 9, 10)]
        return lax.while_loop(go, more, (jnp.int32(REACH), near, far, acc))[3].astype(BF16)

    small = lax.cond(longest > REACH, extend, lambda acc, small: small, acc, small)
    back = lax.all_to_all(small.reshape(heads, rows, 3 * PAIR), "heads", split_axis=0, concat_axis=0)
    out = jax.ShapeDtypeStruct((rows, heads * PAIR), F32)
    return tuple(call(unpack_body, (out, out, out), [VMEM], (VMEM,) * 3, 1 << 20, name="unpack")(back))


def solution(mesh):
    tokens = P(("seq", "heads"), None)
    in_specs = (
        tokens, tokens, tokens, tokens, P("seq", None, "heads"), P("seq", "heads"),
        P("seq", "heads"), P(), P(), P("seq"),
    )
    return jax.shard_map(
        body, mesh=mesh, in_specs=in_specs, out_specs=(tokens,) * 3, check_vma=False
    )
```

```python
import functools
import math

import jax
import jax.numpy as jnp
from jax import lax
from jax.experimental import pallas as pl
from jax.experimental.pallas import tpu as pltpu
from jax.sharding import PartitionSpec as P

HEAD = 64
PAIR = 128
TOK = 256
FEAT = 2080
SHARDS = 32
ROW = 8
COLS = SHARDS // ROW
REACH = 10
F32 = jnp.float32
BF16 = jnp.bfloat16
I32 = jnp.int32

VMEM = pl.BlockSpec(memory_space=pltpu.VMEM)
SMEM = pl.BlockSpec(memory_space=pltpu.SMEM)


def call(body, out_shape, in_specs, out_specs, flops, scratch=(), aliases=None, name=None,
         vmem=24):
    return pl.pallas_call(
        body,
        out_shape=out_shape,
        in_specs=in_specs,
        out_specs=out_specs,
        scratch_shapes=list(scratch),
        input_output_aliases=aliases or {},
        compiler_params=pltpu.CompilerParams(vmem_limit_bytes=vmem * 1024 * 1024),
        cost_estimate=pl.CostEstimate(flops=flops, bytes_accessed=1 << 20, transcendentals=0),
        name=name,
    )


def dot_nt(a, b):
    return lax.dot_general(a, b, (((1,), (1,)), ((), ())), preferred_element_type=F32)


def dot_tn(a, b):
    return lax.dot_general(a, b, (((0,), (0,)), ((), ())), preferred_element_type=F32)


def dot_nn(a, b):
    return lax.dot_general(a, b, (((1,), (0,)), ((), ())), preferred_element_type=F32)


def by_head(x):
    low = lax.broadcasted_iota(I32, x.shape, 1) < HEAD
    zero = jnp.zeros_like(x)
    return jnp.where(low, x, zero), jnp.where(low, zero, x)


def attend(q, g, keys, values, lo, hi):
    place = lax.broadcasted_iota(I32, (TOK, q.shape[0]), 0)
    seen = (place >= lo) & (place <= hi)
    slopes, squares = [], []
    for k, v in zip(by_head(keys), by_head(values)):
        score = jnp.where(seen, dot_nt(k, q), 0.0)
        inner = dot_nt(v, g)
        slopes.append((2.0 * score * inner).astype(BF16))
        squares.append((score * score).astype(BF16))
    slope = jnp.concatenate(slopes, 1)
    square = jnp.concatenate(squares, 1)
    k_part = dot_nn(slope, jnp.concatenate(by_head(q), 0))
    v_part = dot_nn(square, jnp.concatenate(by_head(g), 0))
    return slopes, k_part, v_part


def pack_body(start, q, g, k, v, vq, vg, out, msg, buf, sems):
    copies = [
        pltpu.make_async_copy(ref, buf.at[n], sems.at[n]) for n, ref in enumerate((q, g, k, v))
    ]
    for copy in copies:
        copy.start()
    top = jnp.concatenate([vq[...], vg[...]], 1).astype(F32)
    low = jnp.full((8, 2 * PAIR), start[0].astype(F32))
    msg[...] = jnp.concatenate([top, low], 0).astype(BF16)
    for n, copy in enumerate(copies):
        copy.wait()
        for h in range(out.shape[0]):
            out[h, :, n * PAIR : (n + 1) * PAIR] = buf[n, :, h * PAIR : (h + 1) * PAIR]


def unpack_body(x, qo, ko, vo):
    for h in range(x.shape[0]):
        for n, ref in enumerate((qo, ko, vo)):
            ref[:, h * PAIR : (h + 1) * PAIR] = x[h, :, n * PAIR : (n + 1) * PAIR].astype(F32)


def assemble_body(t, *rest):
    msgs, (block, rows) = rest[:COLS], rest[COLS:]
    x = lax.div(lax.axis_index("seq"), ROW)
    block[0:TOK, :] = t[:, 0 : 2 * PAIR]
    group = lax.shift_right_logical(lax.broadcasted_iota(I32, (16, 2 * PAIR), 0), 2)
    starts = jnp.zeros((16, 2 * PAIR), F32)
    for dx, msg in enumerate(msgs):
        at = lax.rem(x + dx, COLS)
        piece = msg[...].astype(F32)
        rows[pl.ds(pl.multiple_of(at * 8, 8), 8), :] = piece[0:8, :]
        starts = jnp.where(group == at, piece[8:9, :], starts)
    block[TOK : TOK + 32, :] = rows[...].astype(BF16)
    block[TOK + 32 : TOK + 48, :] = starts.astype(BF16)


def own_body(start_ref, owner, place, t, acc, who):
    who[0:1, :] = owner[...]
    who[1:2, :] = place[...]
    start = start_ref[0]
    spot = lax.broadcasted_iota(I32, (1, TOK), 1)
    lo = jnp.where(spot >= start, start, 0)
    q, g, k, v = (t[:, n * PAIR : (n + 1) * PAIR] for n in range(4))
    slopes, k_part, v_part = attend(q, g, k, v, lo, spot)
    k0, k1 = by_head(k)
    acc[:, 0:PAIR] = dot_tn(slopes[0], k0) + dot_tn(slopes[1], k1)
    acc[:, PAIR : 2 * PAIR] = k_part
    acc[:, 2 * PAIR : 3 * PAIR] = v_part


def state_body(start_ref, m, t, acc_in, acc, pt, qt, rows, res):
    start = start_ref[0]
    chunk = 416
    for h, g in enumerate(by_head(t[:, PAIR : 2 * PAIR])):
        for c in range(0, FEAT, chunk):
            r = dot_nt(m[c : c + chunk, :], g)
            pt[2 * h, c : c + chunk, :] = r[:, 0:PAIR]
            pt[2 * h + 1, c : c + chunk, :] = r[:, PAIR : 2 * PAIR]
    q_t = t[:, 0:PAIR].astype(F32).T
    for h in range(2):
        for half in range(2):
            qt[2 * h + half] = q_t[h * HEAD : (h + 1) * HEAD, half * PAIR : (half + 1) * PAIR]
    sub = lax.broadcasted_iota(I32, (8, PAIR), 0)

    def part(i, carry):
        tiles = HEAD // 8
        sums = [jnp.zeros((8, PAIR), F32) for _ in range(tiles)]
        for a in range(HEAD):
            first = a // 8
            at = a * HEAD - a * (a - 1) // 2 - a % 8
            qa = qt[i, a : a + 1, :]
            row = None
            for b in range(first, tiles):
                tile = pt[i, at + 8 * (b - first) : at + 8 * (b - first) + 8, :]
                if b == first:
                    scale = jnp.where(sub > a % 8, 1.0, jnp.where(sub == a % 8, math.sqrt(0.5), 0.0))
                    tile = tile * scale
                sums[b] = sums[b] + tile * qa
                more = tile * qt[i, 8 * b : 8 * b + 8, :]
                row = more if row is None else row + more
            rows[i, a : a + 1, :] = jnp.sum(row, axis=0, keepdims=True)
        for b in range(tiles):
            res[i, 8 * b : 8 * b + 8, :] = math.sqrt(2.0) * (sums[b] + rows[i, 8 * b : 8 * b + 8, :])
        return carry

    lax.fori_loop(0, 4, part, 0)
    for half in range(2):
        both = jnp.concatenate([res[half], res[2 + half]], 0).T
        spot = half * PAIR + lax.broadcasted_iota(I32, (PAIR, PAIR), 0)
        at = slice(half * PAIR, (half + 1) * PAIR)
        acc[at, 0:PAIR] = acc_in[at, 0:PAIR] + jnp.where(spot < start, both, 0.0)
    acc[:, PAIR : 3 * PAIR] = acc_in[:, PAIR : 3 * PAIR]


def later_part(far, start, t, block):
    x = lax.rem(lax.div(lax.axis_index("seq") + far, ROW), COLS)
    group = lax.shift_right_logical(lax.broadcasted_iota(I32, (16, 2 * PAIR), 0), 2)
    begin = block[TOK + 32 : TOK + 48, :].astype(F32)
    until = jnp.max(jnp.where(group == x, begin, 0.0), axis=0, keepdims=True).astype(I32)
    spot = lax.broadcasted_iota(I32, (1, TOK), 1)
    lo = jnp.where(start == TOK, 0, start)
    hi = jnp.where(spot < until, TOK - 1, -1)
    k, v = t[:, 2 * PAIR : 3 * PAIR], t[:, 3 * PAIR : 4 * PAIR]
    q, g = block[0:TOK, 0:PAIR], block[0:TOK, PAIR : 2 * PAIR]
    _, k_part, v_part = attend(q, g, k, v, lo, hi)
    return k_part, v_part


def later_body(fars, start_ref, t, *rest):
    blocks, out = rest[:-1], rest[-1]
    for n, (far, block) in enumerate(zip(fars, blocks)):
        k_part, v_part = later_part(far, start_ref[0], t, block)
        out[n, :, 0:PAIR] = k_part
        out[n, :, PAIR : 2 * PAIR] = v_part


def add_later(far, count, start, t, block, acc):
    @pl.when(far <= count)
    def _():
        k_part, v_part = later_part(far, start, t, block)
        acc[:, PAIR : 2 * PAIR] += k_part
        acc[:, 2 * PAIR : 3 * PAIR] += v_part


def final_body(done, rest_fars, start_ref, who, t, acc_in, *refs):
    refs = list(refs)
    columns = [refs.pop(0) for _ in range(ROW)]
    parts = [refs.pop(0) for _ in done]
    blocks = [refs.pop(0) for _ in rest_fars]
    acc, small, longest, count, rows, starts = refs
    shard = lax.axis_index("seq")
    start = start_ref[0]
    z = lax.rem(shard, ROW)
    for block, dz in zip(columns, range(ROW)):
        piece = block[TOK : TOK + 48, :].astype(F32)
        zz = lax.rem(z + dz, ROW)
        for x in range(COLS):
            at = x * ROW + zz
            rows[pl.ds(pl.multiple_of(at * 8, 8), 8), :] = piece[8 * x : 8 * x + 8, :]
            starts[pl.ds(at, 1), :] = piece[32 + 4 * x : 33 + 4 * x, :]
    begin = starts[...]
    sub = lax.broadcasted_iota(I32, (SHARDS, TOK), 0)
    lane = lax.broadcasted_iota(I32, (SHARDS, TOK), 1)
    along = jnp.sum(jnp.where(sub == lane, begin, 0.0), axis=0, keepdims=True)
    stops = (lane > sub) & (lane < SHARDS) & (along < TOK)
    last = jnp.min(jnp.where(stops, lane, SHARDS - 1).astype(F32), axis=1, keepdims=True)
    sub1 = lax.broadcasted_iota(I32, (SHARDS, 1), 0)
    longest[0] = jnp.max(last - sub1.astype(F32)).astype(I32)
    mine = jnp.sum(jnp.where(sub1 == shard, last, 0.0)).astype(I32)
    reach = mine - shard
    count[0] = reach
    owner = who[0:1, :]
    place = who[1:2, :]
    theirs = jnp.sum(jnp.where(sub == owner, begin, 0.0), axis=0, keepdims=True).astype(I32)
    here = owner == shard
    after = (owner > shard) & (owner <= mine) & (place < theirs)
    carry_lo = jnp.where(start == TOK, 0, start)
    lo = jnp.where(here, jnp.where(place >= start, start, 0), carry_lo)
    hi = jnp.where(here, place, jnp.where(after, TOK - 1, -1))
    both = rows[...].astype(BF16)
    k, v = t[:, 2 * PAIR : 3 * PAIR], t[:, 3 * PAIR : 4 * PAIR]
    _, k_part, v_part = attend(both[:, 0:PAIR], both[:, PAIR:], k, v, lo, hi)
    acc[:, 0:PAIR] = acc_in[:, 0:PAIR]
    acc[:, PAIR : 2 * PAIR] = acc_in[:, PAIR : 2 * PAIR] + k_part
    acc[:, 2 * PAIR : 3 * PAIR] = acc_in[:, 2 * PAIR : 3 * PAIR] + v_part
    for fars, part in zip(done, parts):
        for n, far in enumerate(fars):

            @pl.when(far <= reach)
            def _():
                acc[:, PAIR : 3 * PAIR] += part[n]

    for far, block in zip(rest_fars, blocks):
        add_later(far, reach, start, t, block, acc)
    small[...] = acc[...].astype(BF16)


def further_body(start_ref, count, base, t, acc_in, *rest):
    blocks, acc = rest[:-1], rest[-1]
    acc[...] = acc_in[...]
    for n, block in enumerate(blocks):
        add_later(base[0] + n + 1, count[0], start_ref[0], t, block, acc)


ACC = jax.ShapeDtypeStruct((TOK, 3 * PAIR), F32)
BLOCK = jax.ShapeDtypeStruct((TOK + 48, 2 * PAIR), BF16)
BLOCK_FLOPS = 8 * 2 * TOK * TOK * PAIR


def later_call(fars, start, t, blocks):
    return call(
        functools.partial(later_body, fars),
        jax.ShapeDtypeStruct((len(fars), TOK, 2 * PAIR), F32),
        [SMEM] + [VMEM] * (1 + len(fars)), VMEM, BLOCK_FLOPS * len(fars), name="later",
    )(start, t, *blocks)


def further_call(start, count, base, t, acc, blocks):
    return call(
        further_body, ACC, [SMEM, SMEM, SMEM] + [VMEM] * (2 + len(blocks)), VMEM,
        BLOCK_FLOPS * len(blocks), aliases={4: 0}, name="further",
    )(start, count, base, t, acc, *blocks)


def shift(x, d):
    return lax.ppermute(x, "seq", [((i + d) % SHARDS, i) for i in range(SHARDS)])


def body(
    queries, keys, values, out_grad, prefix_state, variant_queries, variant_grads,
    variant_owner, variant_position, start,
):
    heads = queries.shape[1] // PAIR
    rows = queries.shape[0]
    anywhere = pl.BlockSpec(memory_space=pltpu.HBM)
    sent, msg = call(
        pack_body,
        (
            jax.ShapeDtypeStruct((heads, rows, 4 * PAIR), BF16),
            jax.ShapeDtypeStruct((16, 2 * PAIR), BF16),
        ),
        [SMEM] + [anywhere] * 4 + [VMEM] * 2, (VMEM, VMEM), 1 << 20,
        scratch=(pltpu.VMEM((4, rows, heads * PAIR), BF16), pltpu.SemaphoreType.DMA((4,))),
        name="pack", vmem=60,
    )(start, queries, out_grad, keys, values, variant_queries, variant_grads)
    msgs = [msg] + [shift(msg, ROW * d) for d in range(1, COLS)]
    t = lax.all_to_all(sent, "heads", split_axis=0, concat_axis=0).reshape(TOK, 4 * PAIR)
    own = call(
        assemble_body, BLOCK, [VMEM] * (1 + COLS), VMEM, 1 << 20,
        scratch=(pltpu.VMEM((32, 2 * PAIR), F32),), name="assemble",
    )(t, *msgs)

    blocks = {far: shift(own, far) for far in (7, 2, 8, 1)}
    for far, via in ((5, 7), (6, 7), (4, 2), (3, 2)):
        blocks[far] = shift(blocks[via], far - via)
    acc, who = call(
        own_body, (ACC, jax.ShapeDtypeStruct((8, TOK), I32)), [SMEM, VMEM, VMEM, VMEM],
        (VMEM, VMEM), BLOCK_FLOPS * 3 // 2, name="own",
    )(start, variant_owner.reshape(1, TOK), variant_position.reshape(1, TOK), t)
    acc = call(
        state_body, ACC, [SMEM, VMEM, VMEM, VMEM], VMEM, 3 * BLOCK_FLOPS,
        scratch=(
            pltpu.VMEM((4, FEAT, PAIR), F32),
            pltpu.VMEM((4, HEAD, PAIR), F32),
            pltpu.VMEM((4, HEAD, PAIR), F32),
            pltpu.VMEM((4, HEAD, PAIR), F32),
        ),
        aliases={3: 0}, name="state",
    )(start, prefix_state[0], t, acc)
    near, second = lax.optimization_barrier((blocks[1], blocks[2]))
    blocks[9], blocks[10] = shift(near, ROW), shift(second, ROW)
    done = ((1, 8), (2, 7), (4, 5))
    parts = [later_call(fars, start, t, [blocks[far] for far in fars]) for fars in done]
    left = (3, 6, 9, 10)
    one = jax.ShapeDtypeStruct((1,), I32)
    columns = [own] + [blocks[far] for far in range(1, ROW)]
    acc, small, longest, count = call(
        functools.partial(final_body, done, left),
        (ACC, jax.ShapeDtypeStruct(ACC.shape, BF16), one, one),
        [SMEM] + [VMEM] * (3 + ROW + len(done) + len(left)), (VMEM, VMEM, SMEM, SMEM),
        BLOCK_FLOPS,
        scratch=(pltpu.VMEM((TOK, 2 * PAIR), F32), pltpu.VMEM((SHARDS, 2 * PAIR), F32)),
        aliases={3: 0}, name="final",
    )(
        start, who, t, acc,
        *columns, *parts, *[blocks[far] for far in left],
    )
    longest = longest.reshape(())

    def extend(acc, small):
        def go(carry):
            return carry[0] < longest

        def more(carry):
            base, near, far, acc = carry
            moved = [shift(block, ROW) for block in near]
            acc = further_call(start, count, base.reshape(1), t, acc, moved)
            return base + len(near), far, moved, acc

        near = [blocks[n] for n in (3, 4, 5, 6)]
        far = [blocks[n] for n in (7, 8, 9, 10)]
        return lax.while_loop(go, more, (jnp.int32(REACH), near, far, acc))[3].astype(BF16)

    small = lax.cond(longest > REACH, extend, lambda acc, small: small, acc, small)
    back = lax.all_to_all(small.reshape(heads, rows, 3 * PAIR), "heads", split_axis=0, concat_axis=0)
    out = jax.ShapeDtypeStruct((rows, heads * PAIR), F32)
    return tuple(call(unpack_body, (out, out, out), [VMEM], (VMEM,) * 3, 1 << 20, name="unpack")(back))


def solution(mesh):
    tokens = P(("seq", "heads"), None)
    in_specs = (
        tokens, tokens, tokens, tokens, P("seq", None, "heads"), P("seq", "heads"),
        P("seq", "heads"), P(), P(), P("seq"),
    )
    return jax.shard_map(
        body, mesh=mesh, in_specs=in_specs, out_specs=(tokens,) * 3, check_vma=False
    )
```

```python
import functools
import math

import jax
import jax.numpy as jnp
from jax import lax
from jax.experimental import pallas as pl
from jax.experimental.pallas import tpu as pltpu
from jax.sharding import PartitionSpec as P

HEAD = 64
PAIR = 128
TOK = 256
FEAT = 2080
SHARDS = 32
ROW = 8
COLS = SHARDS // ROW
REACH = 10
F32 = jnp.float32
BF16 = jnp.bfloat16
I32 = jnp.int32

VMEM = pl.BlockSpec(memory_space=pltpu.VMEM)
SMEM = pl.BlockSpec(memory_space=pltpu.SMEM)


def call(body, out_shape, in_specs, out_specs, flops, scratch=(), aliases=None, name=None,
         vmem=24):
    return pl.pallas_call(
        body,
        out_shape=out_shape,
        in_specs=in_specs,
        out_specs=out_specs,
        scratch_shapes=list(scratch),
        input_output_aliases=aliases or {},
        compiler_params=pltpu.CompilerParams(vmem_limit_bytes=vmem * 1024 * 1024),
        cost_estimate=pl.CostEstimate(flops=flops, bytes_accessed=1 << 20, transcendentals=0),
        name=name,
    )


def dot_nt(a, b):
    return lax.dot_general(a, b, (((1,), (1,)), ((), ())), preferred_element_type=F32)


def dot_tn(a, b):
    return lax.dot_general(a, b, (((0,), (0,)), ((), ())), preferred_element_type=F32)


def dot_nn(a, b):
    return lax.dot_general(a, b, (((1,), (0,)), ((), ())), preferred_element_type=F32)


def by_head(x):
    low = lax.broadcasted_iota(I32, x.shape, 1) < HEAD
    zero = jnp.zeros_like(x)
    return jnp.where(low, x, zero), jnp.where(low, zero, x)


def attend(q, g, keys, values, lo, hi):
    place = lax.broadcasted_iota(I32, (TOK, q.shape[0]), 0)
    seen = (place >= lo) & (place <= hi)
    slopes, squares = [], []
    for k, v in zip(by_head(keys), by_head(values)):
        score = jnp.where(seen, dot_nt(k, q), 0.0)
        inner = dot_nt(v, g)
        slopes.append((2.0 * score * inner).astype(BF16))
        squares.append((score * score).astype(BF16))
    slope = jnp.concatenate(slopes, 1)
    square = jnp.concatenate(squares, 1)
    k_part = dot_nn(slope, jnp.concatenate(by_head(q), 0))
    v_part = dot_nn(square, jnp.concatenate(by_head(g), 0))
    return slopes, k_part, v_part


def pack_body(start, q, g, k, v, vq, vg, out, msg, buf, sems):
    copies = [
        pltpu.make_async_copy(ref, buf.at[n], sems.at[n]) for n, ref in enumerate((q, g, k, v))
    ]
    for copy in copies:
        copy.start()
    top = jnp.concatenate([vq[...], vg[...]], 1).astype(F32)
    low = jnp.full((8, 2 * PAIR), start[0].astype(F32))
    msg[...] = jnp.concatenate([top, low], 0).astype(BF16)
    for n, copy in enumerate(copies):
        copy.wait()
        for h in range(out.shape[0]):
            out[h, :, n * PAIR : (n + 1) * PAIR] = buf[n, :, h * PAIR : (h + 1) * PAIR]


def unpack_body(x, qo, ko, vo):
    for h in range(x.shape[0]):
        for n, ref in enumerate((qo, ko, vo)):
            ref[:, h * PAIR : (h + 1) * PAIR] = x[h, :, n * PAIR : (n + 1) * PAIR].astype(F32)


def assemble_body(t, *rest):
    msgs, (block, rows) = rest[:COLS], rest[COLS:]
    x = lax.div(lax.axis_index("seq"), ROW)
    block[0:TOK, :] = t[:, 0 : 2 * PAIR]
    group = lax.shift_right_logical(lax.broadcasted_iota(I32, (16, 2 * PAIR), 0), 2)
    starts = jnp.zeros((16, 2 * PAIR), F32)
    for dx, msg in enumerate(msgs):
        at = lax.rem(x + dx, COLS)
        piece = msg[...].astype(F32)
        rows[pl.ds(pl.multiple_of(at * 8, 8), 8), :] = piece[0:8, :]
        starts = jnp.where(group == at, piece[8:9, :], starts)
    block[TOK : TOK + 32, :] = rows[...].astype(BF16)
    block[TOK + 32 : TOK + 48, :] = starts.astype(BF16)


def own_body(start_ref, owner, place, t, acc, who):
    who[0:1, :] = owner[...]
    who[1:2, :] = place[...]
    start = start_ref[0]
    spot = lax.broadcasted_iota(I32, (1, TOK), 1)
    lo = jnp.where(spot >= start, start, 0)
    q, g, k, v = (t[:, n * PAIR : (n + 1) * PAIR] for n in range(4))
    slopes, k_part, v_part = attend(q, g, k, v, lo, spot)
    k0, k1 = by_head(k)
    acc[:, 0:PAIR] = dot_tn(slopes[0], k0) + dot_tn(slopes[1], k1)
    acc[:, PAIR : 2 * PAIR] = k_part
    acc[:, 2 * PAIR : 3 * PAIR] = v_part


def state_body(start_ref, m, t, acc_in, acc, pt, qt, rows, res):
    start = start_ref[0]
    chunk = 416
    for h, g in enumerate(by_head(t[:, PAIR : 2 * PAIR])):
        for c in range(0, FEAT, chunk):
            r = dot_nt(m[c : c + chunk, :], g)
            pt[2 * h, c : c + chunk, :] = r[:, 0:PAIR]
            pt[2 * h + 1, c : c + chunk, :] = r[:, PAIR : 2 * PAIR]
    q_t = t[:, 0:PAIR].astype(F32).T
    for h in range(2):
        for half in range(2):
            qt[2 * h + half] = q_t[h * HEAD : (h + 1) * HEAD, half * PAIR : (half + 1) * PAIR]
    sub = lax.broadcasted_iota(I32, (8, PAIR), 0)

    def part(i, carry):
        tiles = HEAD // 8
        sums = [jnp.zeros((8, PAIR), F32) for _ in range(tiles)]
        for a in range(HEAD):
            first = a // 8
            at = a * HEAD - a * (a - 1) // 2 - a % 8
            qa = qt[i, a : a + 1, :]
            row = None
            for b in range(first, tiles):
                tile = pt[i, at + 8 * (b - first) : at + 8 * (b - first) + 8, :]
                if b == first:
                    scale = jnp.where(sub > a % 8, 1.0, jnp.where(sub == a % 8, math.sqrt(0.5), 0.0))
                    tile = tile * scale
                sums[b] = sums[b] + tile * qa
                more = tile * qt[i, 8 * b : 8 * b + 8, :]
                row = more if row is None else row + more
            rows[i, a : a + 1, :] = jnp.sum(row, axis=0, keepdims=True)
        for b in range(tiles):
            res[i, 8 * b : 8 * b + 8, :] = math.sqrt(2.0) * (sums[b] + rows[i, 8 * b : 8 * b + 8, :])
        return carry

    lax.fori_loop(0, 4, part, 0)
    for half in range(2):
        both = jnp.concatenate([res[half], res[2 + half]], 0).T
        spot = half * PAIR + lax.broadcasted_iota(I32, (PAIR, PAIR), 0)
        at = slice(half * PAIR, (half + 1) * PAIR)
        acc[at, 0:PAIR] = acc_in[at, 0:PAIR] + jnp.where(spot < start, both, 0.0)
    acc[:, PAIR : 3 * PAIR] = acc_in[:, PAIR : 3 * PAIR]


def later_part(far, start, t, block):
    x = lax.rem(lax.div(lax.axis_index("seq") + far, ROW), COLS)
    group = lax.shift_right_logical(lax.broadcasted_iota(I32, (16, 2 * PAIR), 0), 2)
    begin = block[TOK + 32 : TOK + 48, :].astype(F32)
    until = jnp.max(jnp.where(group == x, begin, 0.0), axis=0, keepdims=True).astype(I32)
    spot = lax.broadcasted_iota(I32, (1, TOK), 1)
    lo = jnp.where(start == TOK, 0, start)
    hi = jnp.where(spot < until, TOK - 1, -1)
    k, v = t[:, 2 * PAIR : 3 * PAIR], t[:, 3 * PAIR : 4 * PAIR]
    q, g = block[0:TOK, 0:PAIR], block[0:TOK, PAIR : 2 * PAIR]
    _, k_part, v_part = attend(q, g, k, v, lo, hi)
    return k_part, v_part


def later_body(fars, start_ref, t, *rest):
    blocks, out = rest[:-1], rest[-1]
    for n, (far, block) in enumerate(zip(fars, blocks)):
        k_part, v_part = later_part(far, start_ref[0], t, block)
        out[n, :, 0:PAIR] = k_part
        out[n, :, PAIR : 2 * PAIR] = v_part


def add_later(far, count, start, t, block, acc):
    @pl.when(far <= count)
    def _():
        k_part, v_part = later_part(far, start, t, block)
        acc[:, PAIR : 2 * PAIR] += k_part
        acc[:, 2 * PAIR : 3 * PAIR] += v_part


def final_body(done, rest_fars, start_ref, who, t, acc_in, *refs):
    refs = list(refs)
    columns = [refs.pop(0) for _ in range(ROW)]
    parts = [refs.pop(0) for _ in done]
    blocks = [refs.pop(0) for _ in rest_fars]
    acc, small, longest, count, rows, starts = refs
    shard = lax.axis_index("seq")
    start = start_ref[0]
    z = lax.rem(shard, ROW)
    for block, dz in zip(columns, range(ROW)):
        piece = block[TOK : TOK + 48, :].astype(F32)
        zz = lax.rem(z + dz, ROW)
        for x in range(COLS):
            at = x * ROW + zz
            rows[pl.ds(pl.multiple_of(at * 8, 8), 8), :] = piece[8 * x : 8 * x + 8, :]
            starts[pl.ds(at, 1), :] = piece[32 + 4 * x : 33 + 4 * x, :]
    begin = starts[...]
    sub = lax.broadcasted_iota(I32, (SHARDS, TOK), 0)
    lane = lax.broadcasted_iota(I32, (SHARDS, TOK), 1)
    along = jnp.sum(jnp.where(sub == lane, begin, 0.0), axis=0, keepdims=True)
    stops = (lane > sub) & (lane < SHARDS) & (along < TOK)
    last = jnp.min(jnp.where(stops, lane, SHARDS - 1).astype(F32), axis=1, keepdims=True)
    sub1 = lax.broadcasted_iota(I32, (SHARDS, 1), 0)
    longest[0] = jnp.max(last - sub1.astype(F32)).astype(I32)
    mine = jnp.sum(jnp.where(sub1 == shard, last, 0.0)).astype(I32)
    reach = mine - shard
    count[0] = reach
    owner = who[0:1, :]
    place = who[1:2, :]
    theirs = jnp.sum(jnp.where(sub == owner, begin, 0.0), axis=0, keepdims=True).astype(I32)
    here = owner == shard
    after = (owner > shard) & (owner <= mine) & (place < theirs)
    carry_lo = jnp.where(start == TOK, 0, start)
    lo = jnp.where(here, jnp.where(place >= start, start, 0), carry_lo)
    hi = jnp.where(here, place, jnp.where(after, TOK - 1, -1))
    both = rows[...].astype(BF16)
    k, v = t[:, 2 * PAIR : 3 * PAIR], t[:, 3 * PAIR : 4 * PAIR]
    _, k_part, v_part = attend(both[:, 0:PAIR], both[:, PAIR:], k, v, lo, hi)
    acc[:, 0:PAIR] = acc_in[:, 0:PAIR]
    acc[:, PAIR : 2 * PAIR] = acc_in[:, PAIR : 2 * PAIR] + k_part
    acc[:, 2 * PAIR : 3 * PAIR] = acc_in[:, 2 * PAIR : 3 * PAIR] + v_part
    for fars, part in zip(done, parts):
        for n, far in enumerate(fars):

            @pl.when(far <= reach)
            def _():
                acc[:, PAIR : 3 * PAIR] += part[n]

    for far, block in zip(rest_fars, blocks):
        add_later(far, reach, start, t, block, acc)
    small[...] = acc[...].astype(BF16)


def further_body(start_ref, count, base, t, acc_in, *rest):
    blocks, acc = rest[:-1], rest[-1]
    acc[...] = acc_in[...]
    for n, block in enumerate(blocks):
        add_later(base[0] + n + 1, count[0], start_ref[0], t, block, acc)


ACC = jax.ShapeDtypeStruct((TOK, 3 * PAIR), F32)
BLOCK = jax.ShapeDtypeStruct((TOK + 48, 2 * PAIR), BF16)
BLOCK_FLOPS = 8 * 2 * TOK * TOK * PAIR


def later_call(fars, start, t, blocks):
    return call(
        functools.partial(later_body, fars),
        jax.ShapeDtypeStruct((len(fars), TOK, 2 * PAIR), F32),
        [SMEM] + [VMEM] * (1 + len(fars)), VMEM, BLOCK_FLOPS * len(fars), name="later",
    )(start, t, *blocks)


def further_call(start, count, base, t, acc, blocks):
    return call(
        further_body, ACC, [SMEM, SMEM, SMEM] + [VMEM] * (2 + len(blocks)), VMEM,
        BLOCK_FLOPS * len(blocks), aliases={4: 0}, name="further",
    )(start, count, base, t, acc, *blocks)


def shift(x, d):
    return lax.ppermute(x, "seq", [((i + d) % SHARDS, i) for i in range(SHARDS)])


def body(
    queries, keys, values, out_grad, prefix_state, variant_queries, variant_grads,
    variant_owner, variant_position, start,
):
    heads = queries.shape[1] // PAIR
    rows = queries.shape[0]
    anywhere = pl.BlockSpec(memory_space=pltpu.HBM)
    sent, msg = call(
        pack_body,
        (
            jax.ShapeDtypeStruct((heads, rows, 4 * PAIR), BF16),
            jax.ShapeDtypeStruct((16, 2 * PAIR), BF16),
        ),
        [SMEM] + [anywhere] * 4 + [VMEM] * 2, (VMEM, VMEM), 1 << 20,
        scratch=(pltpu.VMEM((4, rows, heads * PAIR), BF16), pltpu.SemaphoreType.DMA((4,))),
        name="pack", vmem=60,
    )(start, queries, out_grad, keys, values, variant_queries, variant_grads)
    msgs = [msg] + [shift(msg, ROW * d) for d in range(1, COLS)]
    t = lax.all_to_all(sent, "heads", split_axis=0, concat_axis=0).reshape(TOK, 4 * PAIR)
    own = call(
        assemble_body, BLOCK, [VMEM] * (1 + COLS), VMEM, 1 << 20,
        scratch=(pltpu.VMEM((32, 2 * PAIR), F32),), name="assemble",
    )(t, *msgs)

    blocks = {far: shift(own, far) for far in (7, 2, 8, 1)}
    for far, via in ((5, 7), (6, 7), (4, 2), (3, 2)):
        blocks[far] = shift(blocks[via], far - via)
    acc, who = call(
        own_body, (ACC, jax.ShapeDtypeStruct((8, TOK), I32)), [SMEM, VMEM, VMEM, VMEM],
        (VMEM, VMEM), BLOCK_FLOPS * 3 // 2, name="own",
    )(start, variant_owner.reshape(1, TOK), variant_position.reshape(1, TOK), t)
    acc = call(
        state_body, ACC, [SMEM, VMEM, VMEM, VMEM], VMEM, 3 * BLOCK_FLOPS,
        scratch=(
            pltpu.VMEM((4, FEAT, PAIR), F32),
            pltpu.VMEM((4, HEAD, PAIR), F32),
            pltpu.VMEM((4, HEAD, PAIR), F32),
            pltpu.VMEM((4, HEAD, PAIR), F32),
        ),
        aliases={3: 0}, name="state",
    )(start, prefix_state[0], t, acc)
    near, second = lax.optimization_barrier((blocks[1], blocks[2]))
    blocks[9], blocks[10] = shift(near, ROW), shift(second, ROW)
    done = ((1, 8), (2, 7), (4, 6), (5, 3))
    parts = [later_call(fars, start, t, [blocks[far] for far in fars]) for fars in done]
    left = (9, 10)
    one = jax.ShapeDtypeStruct((1,), I32)
    columns = [own] + [blocks[far] for far in range(1, ROW)]
    acc, small, longest, count = call(
        functools.partial(final_body, done, left),
        (ACC, jax.ShapeDtypeStruct(ACC.shape, BF16), one, one),
        [SMEM] + [VMEM] * (3 + ROW + len(done) + len(left)), (VMEM, VMEM, SMEM, SMEM),
        BLOCK_FLOPS,
        scratch=(pltpu.VMEM((TOK, 2 * PAIR), F32), pltpu.VMEM((SHARDS, 2 * PAIR), F32)),
        aliases={3: 0}, name="final",
    )(
        start, who, t, acc,
        *columns, *parts, *[blocks[far] for far in left],
    )
    longest = longest.reshape(())

    def extend(acc, small):
        def go(carry):
            return carry[0] < longest

        def more(carry):
            base, near, far, acc = carry
            moved = [shift(block, ROW) for block in near]
            acc = further_call(start, count, base.reshape(1), t, acc, moved)
            return base + len(near), far, moved, acc

        near = [blocks[n] for n in (3, 4, 5, 6)]
        far = [blocks[n] for n in (7, 8, 9, 10)]
        return lax.while_loop(go, more, (jnp.int32(REACH), near, far, acc))[3].astype(BF16)

    small = lax.cond(longest > REACH, extend, lambda acc, small: small, acc, small)
    back = lax.all_to_all(small.reshape(heads, rows, 3 * PAIR), "heads", split_axis=0, concat_axis=0)
    out = jax.ShapeDtypeStruct((rows, heads * PAIR), F32)
    return tuple(call(unpack_body, (out, out, out), [VMEM], (VMEM,) * 3, 1 << 20, name="unpack")(back))


def solution(mesh):
    tokens = P(("seq", "heads"), None)
    in_specs = (
        tokens, tokens, tokens, tokens, P("seq", None, "heads"), P("seq", "heads"),
        P("seq", "heads"), P(), P(), P("seq"),
    )
    return jax.shard_map(
        body, mesh=mesh, in_specs=in_specs, out_specs=(tokens,) * 3, check_vma=False
    )
```
